32 devices in a mesh: shot: 2 (over y), slab: 4 (over z), rep: 2 (over x), sub: 2 (over core).
Axes of the slice: x: 2, y: 2, z: 4, core: 2. Of those that a mesh axis runs over, the one named last changes fastest.
Arguments:
- courant: float32 [16, 32, 256], P('slab', 'sub'), may hold values from 0.2 to 0.42
- incident_prev: float32 [32, 32, 256], P(('shot', 'slab'), 'sub', 'rep'), parts along dimension 0, may hold values from -6 to 6
- incident_now: float32 [32, 32, 256], P(('shot', 'slab'), 'sub', 'rep'), parts along dimension 0, may hold values from -6 to 6
- wavelet: float32 [4, 8], replicated, may hold values from -6 to 6
- source_z: int32 [16], P('shot'), parts along dimension 0, may hold values from 0 to 15
- source_y: int32 [16], P('shot'), parts along dimension 0, may hold values from 0 to 31
- source_x: int32 [16], P('shot'), parts along dimension 0, may hold values from 0 to 255
- replica_seeds: int32 [4], P('rep'), may hold values from 0 to 999999
- receiver_z: int32 [32], replicated, may hold values from 0 to 15, as said below
- receiver_y: int32 [32], replicated, may hold values from 0 to 31, as said below
- receiver_x: int32 [32], replicated, may hold values from 0 to 255, as said below
Outputs:
- incident_final: float32 [32, 32, 256], P(('shot', 'slab'), 'sub', 'rep'), parts along dimension 0
- scattered_final: float32 [4, 32, 32, 256], P('rep', ('shot', 'slab'), 'sub'), parts along dimension 1
- traces: float32 [8, 4, 32], P('shot', 'rep'), parts along dimension 0
The draws below stay inside these ranges and needn't reach their ends.
There are 2 independent parts, one for each index of `shot`. The reference program is written for one: setup_inputs(seed, part) draws one part's arguments, and reference() takes and returns one part's arrays. A program takes and returns all parts, laid end to end along the dimension named above; an argument that names none is the same for every part. Nothing has to cross between parts.
Inputs may be any that keep to these rules, and one draw needn't show every extreme that they name: `receiver_z`: receiver j lies at a depth from (j // 8) * 4 to that plus 4 - 1; the first receiver is at depth 0 and the last at depth 16 - 1. `receiver_y`: receiver j lies at a second coordinate from ((j // 4) % 2) * 16 to that plus 16 - 1; the first receiver is at 0 and the last at 31. `receiver_x`: the first receiver is at 0 and the last at 255.
All inputs are finite; a program needn't handle non-finite values.
Results may differ from the reference program's by a relative error of at most 0.00002.
Values sent between devices are 32-bit elements; how exact they have to be, the bound alone decides.
No kernel may reach another device: no remote copies, remote signals or barrier semaphores. Data moves between devices by JAX's collectives and lax.ppermute only.
A program may use at most 64 MiB of HBM per device.

```python
import math
import jax
import jax.numpy as jnp
from jax import lax

CZ = 4
CY = 16
NX = 256
STEPS = 4
NSRC = 8
REC_DEV = 4
NZ = 16
NY = 32
REPS = 4
NREC = 32


def draw_receiver_z(key, part):
    index = jnp.arange(NREC, dtype=jnp.int32)
    slab_of = index // (REC_DEV * (NY // CY))
    offsets = jax.random.randint(jax.random.fold_in(key, 11), (NREC,), 0, CZ, dtype=jnp.int32)
    offsets = offsets.at[0].set(0).at[NREC - 1].set(CZ - 1)
    return slab_of * CZ + offsets


def draw_receiver_y(key, part):
    index = jnp.arange(NREC, dtype=jnp.int32)
    block_of = index // REC_DEV % (NY // CY)
    offsets = jax.random.randint(jax.random.fold_in(key, 23), (NREC,), 0, CY, dtype=jnp.int32)
    offsets = offsets.at[0].set(0).at[NREC - 1].set(CY - 1)
    return block_of * CY + offsets


def draw_receiver_x(key, part):
    offsets = jax.random.randint(jax.random.fold_in(key, 37), (NREC,), 0, NX, dtype=jnp.int32)
    return offsets.at[0].set(0).at[NREC - 1].set(NX - 1)


def set_ends(result, own_key, smallest, high):
    shape = result.shape
    place = [jax.random.randint(jax.random.fold_in(own_key, axis), (), 0, shape[axis]) for axis in range(len(shape))]
    result = result.at[tuple(place)].set(smallest)
    longest = shape.index(max(shape))
    place[longest] = (place[longest] + 1) % shape[longest]
    return result.at[tuple(place)].set(high)


def levels(rng, dims, shards, least, largest):
    def one(dim, shards_of):
        heights = jax.random.uniform(jax.random.fold_in(jax.random.fold_in(rng, 6), dim), (shards_of,), jnp.float32, least / len(shards), largest / len(shards))
        return jnp.repeat(jnp.exp(heights), dims[dim] // shards_of).reshape((-1,) + (1,) * (len(dims) - dim - 1))

    loudness = one(*shards[0])
    for cut in shards[1:]:
        loudness = loudness * one(*cut)
    return loudness


def normal_values(stream_key, dims, deviation, most, shards=(), held_as=jnp.bfloat16):
    result = deviation * jax.random.normal(stream_key, dims, jnp.float32)
    if shards:
        result = result * levels(stream_key, dims, shards, -0.22, 0.18)
    return jnp.clip(result, -most, most).astype(held_as)


def setup_inputs(seed: int = 0, part: int = 0) -> dict:
    splits = jax.random.split(jax.random.key(seed), 12)
    own_keys = jax.random.split(jax.random.fold_in(splits[11], part), 12)
    courant = jnp.clip(jnp.exp(math.log(0.42) - 0.7419373 * jax.random.uniform(splits[0], (NZ, NY, NX), jnp.float32) ** levels(splits[0], (NZ, NY, NX), ((0, 4), (1, 2)), -0.2, 0.2)), 0.2, 0.42)
    incident_prev = normal_values(own_keys[1], (NZ, NY, NX), 1.0, 6.0, ((0, 4), (1, 2), (2, 2)), jnp.float32)
    incident_now = normal_values(own_keys[2], (NZ, NY, NX), 1.0, 6.0, ((0, 4), (1, 2), (2, 2)), jnp.float32)
    wavelet = normal_values(splits[3], (STEPS, NSRC), 1.0, 6.0, (), jnp.float32)
    source_z = set_ends(jax.random.randint(own_keys[4], (NSRC,), 0, NZ), jax.random.fold_in(own_keys[4], 1), 0, NZ - 1).astype(jnp.int32)
    source_y = set_ends(jax.random.randint(own_keys[5], (NSRC,), 0, NY), jax.random.fold_in(own_keys[5], 1), 0, NY - 1).astype(jnp.int32)
    source_x = set_ends(jax.random.randint(own_keys[6], (NSRC,), 0, NX), jax.random.fold_in(own_keys[6], 1), 0, NX - 1).astype(jnp.int32)
    replica_seeds = set_ends(jax.random.randint(splits[7], (REPS,), 0, 1000000), jax.random.fold_in(splits[7], 1), 0, 999999).astype(jnp.int32)
    receiver_z = draw_receiver_z(jax.random.fold_in(splits[11], 71), part)
    receiver_y = draw_receiver_y(jax.random.fold_in(splits[11], 71), part)
    receiver_x = draw_receiver_x(jax.random.fold_in(splits[11], 71), part)
    return dict(courant=courant, incident_prev=incident_prev, incident_now=incident_now, wavelet=wavelet, source_z=source_z, source_y=source_y, source_x=source_x, replica_seeds=replica_seeds, receiver_z=receiver_z, receiver_y=receiver_y, receiver_x=receiver_x)


stencil_coeffs = (-205.0 / 72.0, 8.0 / 5.0, -1.0 / 5.0, 8.0 / 315.0, -1.0 / 560.0)
pert_scale = 0.2


def laplace(padded):
    deep_count = padded.shape[-3] - 8
    tall_count = padded.shape[-2] - 8
    wide_count = padded.shape[-1] - 8

    def window(shift_z, shift_y, shift_x):
        return padded[..., 4 + shift_z:4 + shift_z + deep_count, 4 + shift_y:4 + shift_y + tall_count, 4 + shift_x:4 + shift_x + wide_count]

    summed = (3.0 * stencil_coeffs[0]) * window(0, 0, 0)
    for offset in range(1, 5):
        couple = window(offset, 0, 0) + window(-offset, 0, 0) + window(0, offset, 0) + window(0, -offset, 0) + window(0, 0, offset) + window(0, 0, -offset)
        summed = summed + stencil_coeffs[offset] * couple
    return summed


def perturbation(seed_values, depth_coord, height_coord, width_coord):
    hashed = (seed_values[:, None, None, None] * 668265263 + depth_coord[None, :, None, None] * 73856093 + height_coord[None, None, :, None] * 19349663 + width_coord[None, None, None, :] * 83492791)
    hashed = jnp.bitwise_xor(hashed, jnp.right_shift(hashed, 15))
    hashed = hashed * 1274126177
    hashed = jnp.bitwise_xor(hashed, jnp.right_shift(hashed, 13))
    fraction = jnp.bitwise_and(hashed, 65535).astype(jnp.float32) / 65535.0
    return pert_scale * (2.0 * fraction - 1.0)


def inject(field, amounts, where_z, where_y, where_x, start_z, start_y, start_x):
    local_z = where_z - start_z
    local_y = where_y - start_y
    local_x = where_x - start_x
    inside = (local_z >= 0) & (local_z < field.shape[0]) & (local_y >= 0) & (local_y < field.shape[1]) & (local_x >= 0) & (local_x < field.shape[2])
    clip_z = jnp.clip(local_z, 0, field.shape[0] - 1).astype(jnp.int32)
    clip_y = jnp.clip(local_y, 0, field.shape[1] - 1).astype(jnp.int32)
    clip_x = jnp.clip(local_x, 0, field.shape[2] - 1).astype(jnp.int32)
    return field.at[clip_z, clip_y, clip_x].add(jnp.where(inside, amounts, jnp.zeros_like(amounts)))


def sample(field, where_z, where_y, where_x, start_z, start_y):
    local_z = where_z - start_z
    local_y = where_y - start_y
    inside = (local_z >= 0) & (local_z < field.shape[1]) & (local_y >= 0) & (local_y < field.shape[2])
    clip_z = jnp.clip(local_z, 0, field.shape[1] - 1).astype(jnp.int32)
    clip_y = jnp.clip(local_y, 0, field.shape[2] - 1).astype(jnp.int32)
    picked = field[:, clip_z, clip_y, where_x.astype(jnp.int32)]
    return jnp.where(inside[None, :], picked, jnp.zeros_like(picked))


def reference(courant, incident_prev, incident_now, wavelet, source_z, source_y, source_x, replica_seeds, receiver_z, receiver_y, receiver_x):
    speed_square = courant * courant
    history = [incident_prev, incident_now]
    for step_index in range(STEPS):
        current = history[-1]
        following = 2.0 * current - history[-2] + speed_square * laplace(jnp.pad(current, 4))
        following = inject(following, wavelet[step_index], source_z, source_y, source_x, 0, 0, 0)
        history.append(following)
    depth_coord = jnp.arange(NZ, dtype=jnp.int32)
    height_coord = jnp.arange(NY, dtype=jnp.int32)
    width_coord = jnp.arange(NX, dtype=jnp.int32)

    def one_replica(seed_value):
        contrast = perturbation(seed_value[None], depth_coord, height_coord, width_coord)[0]
        wave_prev = jnp.zeros(incident_now.shape, jnp.float32)
        wave_now = jnp.zeros(incident_now.shape, jnp.float32)
        recorded = []
        for step_index in range(STEPS):
            source_term = 2.0 * contrast * (history[step_index + 2] - 2.0 * history[step_index + 1] + history[step_index])
            wave_next = 2.0 * wave_now - wave_prev + speed_square * laplace(jnp.pad(wave_now, 4)) + source_term
            recorded.append(sample(wave_next[None], receiver_z, receiver_y, receiver_x, 0, 0)[0])
            wave_prev, wave_now = wave_now, wave_next
        return wave_now, jnp.stack(recorded)

    scattered_final, recorded = lax.map(one_replica, replica_seeds)
    traces = jnp.transpose(recorded, (1, 0, 2))
    return history[-1], scattered_final, traces
```

```python
import jax
import jax.numpy as jnp
import numpy as np
from jax import lax
from jax.experimental import pallas as pl
from jax.experimental.pallas import tpu as pltpu
from jax.sharding import PartitionSpec as P

STEPS = 4
GRID_ROWS = 512


stencil_coeffs = (-205.0 / 72.0, 8.0 / 5.0, -1.0 / 5.0, 8.0 / 315.0, -1.0 / 560.0)
pert_scale = 0.2
whole_coeffs = (-14350, 8064, -1008, 128, -9)
coeff_scale = 5040.0


def padded_2(array, sides, width):
    for axis, dim in sides:
        size, length = (lax.axis_size(axis), array.shape[dim])
        up = [(i, (i + 1) % size) for i in range(size - 1)]
        down = [(j, i) for i, j in up]
        last = lax.slice_in_dim(array, length - width, length, axis=dim)
        first = lax.slice_in_dim(array, 0, width, axis=dim)
        before = lax.ppermute(last, axis, up)
        after = lax.ppermute(first, axis, down)
        array = jnp.concatenate([before, array, after], axis=dim)
    return array


def laplace(padded):
    deep_count = padded.shape[-3] - 8
    tall_count = padded.shape[-2] - 8
    wide_count = padded.shape[-1] - 8

    def window(shift_z, shift_y, shift_x):
        return padded[
            ...,
            4 + shift_z : 4 + shift_z + deep_count,
            4 + shift_y : 4 + shift_y + tall_count,
            4 + shift_x : 4 + shift_x + wide_count,
        ]

    summed = 3.0 * stencil_coeffs[0] * window(0, 0, 0)
    for offset in range(1, 5):
        couple = (
            window(offset, 0, 0)
            + window(-offset, 0, 0)
            + window(0, offset, 0)
            + window(0, -offset, 0)
            + window(0, 0, offset)
            + window(0, 0, -offset)
        )
        summed = summed + stencil_coeffs[offset] * couple
    return summed


def perturbation(seed_values, depth_coord, height_coord, width_coord):
    hashed = (
        seed_values[:, None, None, None] * 668265263
        + depth_coord[None, :, None, None] * 73856093
        + height_coord[None, None, :, None] * 19349663
        + width_coord[None, None, None, :] * 83492791
    )
    hashed = jnp.bitwise_xor(hashed, jnp.right_shift(hashed, 15))
    hashed = hashed * 1274126177
    hashed = jnp.bitwise_xor(hashed, jnp.right_shift(hashed, 13))
    fraction = jnp.bitwise_and(hashed, 65535).astype(jnp.float32) / 65535.0
    return pert_scale * (2.0 * fraction - 1.0)


def inject(field, amounts, where_z, where_y, where_x, start_z, start_y, start_x):
    local_z = where_z - start_z
    local_y = where_y - start_y
    local_x = where_x - start_x
    inside = (
        (local_z >= 0)
        & (local_z < field.shape[0])
        & (local_y >= 0)
        & (local_y < field.shape[1])
        & (local_x >= 0)
        & (local_x < field.shape[2])
    )
    clip_z = jnp.clip(local_z, 0, field.shape[0] - 1)
    clip_y = jnp.clip(local_y, 0, field.shape[1] - 1)
    clip_x = jnp.clip(local_x, 0, field.shape[2] - 1)
    return field.at[clip_z, clip_y, clip_x].add(jnp.where(inside, amounts, jnp.zeros_like(amounts)))


def sample(field, where_z, where_y, where_x, start_z, start_y):
    local_z = where_z - start_z
    local_y = where_y - start_y
    inside = (
        (local_z >= 0) & (local_z < field.shape[1]) & (local_y >= 0) & (local_y < field.shape[2])
    )
    clip_z = jnp.clip(local_z, 0, field.shape[1] - 1)
    clip_y = jnp.clip(local_y, 0, field.shape[2] - 1)
    picked = field[:, clip_z, clip_y, where_x]
    return jnp.where(inside[None, :], picked, jnp.zeros_like(picked))


def halo_shards(
    courant,
    incident_prev,
    incident_now,
    wavelet,
    source_z,
    source_y,
    source_x,
    replica_seeds,
    receiver_z,
    receiver_y,
    receiver_x,
):
    deep_count, tall_count, part_width = incident_now.shape
    full_width = courant.shape[2]
    start_z = lax.axis_index("slab") * deep_count
    start_y = lax.axis_index("sub") * tall_count
    start_x = lax.axis_index("rep") * part_width
    speed_square = courant * courant
    depth_coord = start_z + jnp.arange(deep_count, dtype=jnp.int32)
    height_coord = start_y + jnp.arange(tall_count, dtype=jnp.int32)
    width_coord = jnp.arange(full_width, dtype=jnp.int32)
    contrast = perturbation(replica_seeds, depth_coord, height_coord, width_coord)
    whole_prev, whole_now = (
        lax.all_gather(incident_prev, "rep", axis=2, tiled=True),
        lax.all_gather(incident_now, "rep", axis=2, tiled=True),
    )
    wave_prev = jnp.zeros(contrast.shape, jnp.float32)
    wave_now = jnp.zeros(contrast.shape, jnp.float32)
    recorded = []
    for step_index in range(STEPS):
        padded = padded_2(whole_now, (("slab", 0), ("sub", 1)), 4)
        padded = jnp.pad(padded, ((0, 0), (0, 0), (4, 4)))
        whole_next = 2.0 * whole_now - whole_prev + speed_square * laplace(padded)
        whole_next = inject(
            whole_next, wavelet[step_index], source_z, source_y, source_x, start_z, start_y, 0
        )
        wave_padded = padded_2(wave_now, (("slab", 1), ("sub", 2)), 4)
        wave_padded = jnp.pad(wave_padded, ((0, 0), (0, 0), (0, 0), (4, 4)))
        source_term = 2.0 * contrast * (whole_next - 2.0 * whole_now + whole_prev)
        whole_prev, whole_now = (whole_now, whole_next)
        wave_next = 2.0 * wave_now - wave_prev + speed_square * laplace(wave_padded) + source_term
        picked = sample(wave_next, receiver_z, receiver_y, receiver_x, start_z, start_y)
        picked = lax.psum(picked, ("slab", "sub"))
        recorded.append(picked)
        wave_prev, wave_now = (wave_now, wave_next)
    traces = jnp.stack(recorded)
    incident_final = lax.dynamic_slice_in_dim(whole_now, start_x, part_width, 2)
    return (incident_final, wave_now, traces)


def band(size):
    apart = np.abs(np.arange(size)[:, None] - np.arange(size)[None, :])
    return sum(whole_coeffs[k] * (apart == k) for k in range(1, 5))


def operators(deep, tall, wide):
    rows = np.kron(band(deep), np.eye(tall)) + np.kron(np.eye(deep), band(tall))
    return rows.astype(jnp.bfloat16), band(wide).astype(jnp.bfloat16)


def split3(value):
    high = value.astype(jnp.bfloat16)
    rest = value - high.astype(jnp.float32)
    middle = rest.astype(jnp.bfloat16)
    low = (rest - middle.astype(jnp.float32)).astype(jnp.bfloat16)
    return high, middle, low


def swapped(array, axis, distance):
    size = lax.axis_size(axis)
    return lax.ppermute(array, axis, [(i, i ^ distance) for i in range(size)])


def whole_kernel(
    place_ref,
    wavelet_ref,
    source_ref,
    seeds_ref,
    receiver_ref,
    rows_op_ref,
    wide_op_ref,
    blocks_ref,
    incident_ref,
    scattered_ref,
    traces_ref,
    field_ref,
    speed_ref,
    contrast_ref,
    force_ref,
    drive_ref,
    wave_ref,
    taken_ref,
):
    slab, sub, rep = place_ref[0], place_ref[1], place_ref[2]
    wide_parts, tall_parts, deep_parts, layers, tall_count, part_width = blocks_ref.shape
    deep_count = layers // 3
    deep, tall, wide = deep_parts * deep_count, tall_parts * tall_count, wide_parts * part_width
    rows = deep * tall
    replicas = seeds_ref.shape[0]
    sources = source_ref.shape[1]
    receivers = receiver_ref.shape[1]

    for x in range(wide_parts):
        for y in range(tall_parts):
            for z in range(deep_parts):
                at_z = pl.multiple_of((slab ^ z) * deep_count, deep_count)
                at_y = pl.multiple_of((sub ^ y) * tall_count, tall_count)
                at_x = pl.multiple_of((rep ^ x) * part_width, part_width)
                there = (pl.ds(at_z, deep_count), pl.ds(at_y, tall_count), pl.ds(at_x, part_width))
                block = blocks_ref[x, y, z]
                field_ref[(1,) + there] = block[:deep_count]
                field_ref[(0,) + there] = block[deep_count : 2 * deep_count]
                courant = block[2 * deep_count :]
                speed_ref[there] = courant * courant * (1.0 / coeff_scale)

    z_of = lax.broadcasted_iota(jnp.int32, (deep, tall, wide), 0)
    y_of = lax.broadcasted_iota(jnp.int32, (deep, tall, wide), 1)
    x_of = lax.broadcasted_iota(jnp.int32, (deep, tall, wide), 2)
    cell = z_of * 73856093 + y_of * 19349663 + x_of * 83492791
    for r in range(replicas):
        hashed = cell + seeds_ref[r] * 668265263
        hashed = hashed ^ (hashed >> 15)
        hashed = hashed * 1274126177
        hashed = hashed ^ (hashed >> 13)
        fraction = (hashed & 65535).astype(jnp.float32) / 65535.0
        contrast_ref[r] = 2.0 * (pert_scale * (2.0 * fraction - 1.0))

    lane = lax.broadcasted_iota(jnp.int32, (1, wide), 1)

    force_ref[...] = jnp.zeros_like(force_ref)
    for n in range(STEPS):
        for k in range(sources):
            at = (n, source_ref[0, k], pl.ds(source_ref[1, k], 1), slice(None))
            force_ref[at] += jnp.where(lane == source_ref[2, k], wavelet_ref[n, k], 0.0)

    def applied(value):
        parts = split3(value)
        total = (3.0 * whole_coeffs[0]) * value
        for part in parts:
            total += jnp.dot(rows_op_ref[...], part, preferred_element_type=jnp.float32)
        for part in parts:
            total += jnp.dot(part, wide_op_ref[...], preferred_element_type=jnp.float32)
        return total

    shape = (rows, wide)
    column = lax.broadcasted_iota(jnp.int32, (receivers, 128), 1)
    gathered = jnp.zeros((receivers, 128), jnp.float32)
    speed = speed_ref[...].reshape(shape)
    for n in range(STEPS):
        older, newer = n % 2, (n + 1) % 2
        now = field_ref[newer].reshape(shape)
        drive = speed * applied(now) + force_ref[n].reshape(shape)
        drive_ref[...] = drive
        field_ref[older] = (2.0 * now - field_ref[older].reshape(shape) + drive).reshape(deep, tall, wide)
        for r in range(replicas):
            following = contrast_ref[r].reshape(shape) * drive_ref[...]
            if n > 0:
                wave = wave_ref[newer, r].reshape(shape)
                following += speed * applied(wave) + 2.0 * wave
            if n > 1:
                following -= wave_ref[older, r].reshape(shape)
            wave_ref[older, r] = following.reshape(deep, tall, wide)
            for j in range(receivers):
                row = wave_ref[older, r, receiver_ref[0, j], pl.ds(receiver_ref[1, j], 1), :]
                taken_ref[pl.ds(j, 1), :] = jnp.where(lane == receiver_ref[2, j], row, 0.0)
            summed = jnp.sum(taken_ref[...], axis=1, keepdims=True)
            gathered += jnp.where(column == n * replicas + r, summed, 0.0)
    at_z = pl.multiple_of(slab * deep_count, deep_count)
    at_y = pl.multiple_of(sub * tall_count, tall_count)
    at_x = pl.multiple_of(rep * part_width, part_width)
    own = (pl.ds(at_z, deep_count), pl.ds(at_y, tall_count))
    last = (STEPS - 1) % 2
    incident_ref[...] = field_ref[(last,) + own + (pl.ds(at_x, part_width),)]
    for r in range(replicas):
        scattered_ref[r] = wave_ref[(last, r) + own]
    traces_ref[...] = jnp.transpose(gathered)[: STEPS * replicas, :]


def whole_shards(
    courant,
    incident_prev,
    incident_now,
    wavelet,
    source_z,
    source_y,
    source_x,
    replica_seeds,
    receiver_z,
    receiver_y,
    receiver_x,
):
    deep_count, tall_count, part_width = incident_now.shape
    wide = courant.shape[2]
    slab, sub, rep = (lax.axis_index(axis) for axis in ("slab", "sub", "rep"))
    slabs, subs, reps = (lax.axis_size(axis) for axis in ("slab", "sub", "rep"))
    deep, tall = slabs * deep_count, subs * tall_count
    replicas, receivers = replica_seeds.shape[0], receiver_z.shape[0]
    part = lax.dynamic_slice_in_dim(courant, rep * part_width, part_width, 2)
    own = jnp.concatenate([incident_now, incident_prev, part], axis=0)
    along = {m: swapped(own, "slab", m) for m in sorted(range(1, slabs), key=lambda m: m == 1)}
    blocks = jnp.stack([own] + [along[m] for m in range(1, slabs)])
    blocks = jnp.stack([blocks] + [swapped(blocks, "rep", m) for m in range(1, reps)])
    blocks = jnp.stack([blocks] + [swapped(blocks, "sub", m) for m in range(1, subs)], axis=1)
    rows_op, wide_op = operators(deep, tall, wide)
    smem = pl.BlockSpec(memory_space=pltpu.SMEM)
    vmem = pl.BlockSpec(memory_space=pltpu.VMEM)
    grid = (deep, tall, wide)
    incident_final, scattered_final, traces = pl.pallas_call(
        whole_kernel,
        out_shape=(
            jax.ShapeDtypeStruct((deep_count, tall_count, part_width), jnp.float32),
            jax.ShapeDtypeStruct((replicas, deep_count, tall_count, wide), jnp.float32),
            jax.ShapeDtypeStruct((STEPS * replicas, receivers), jnp.float32),
        ),
        in_specs=[smem] * 5 + [vmem] * 3,
        out_specs=(vmem, vmem, vmem),
        scratch_shapes=[
            pltpu.VMEM((2,) + grid, jnp.float32),
            pltpu.VMEM(grid, jnp.float32),
            pltpu.VMEM((replicas,) + grid, jnp.float32),
            pltpu.VMEM((STEPS,) + grid, jnp.float32),
            pltpu.VMEM((deep * tall, wide), jnp.float32),
            pltpu.VMEM((2, replicas) + grid, jnp.float32),
            pltpu.VMEM((receivers, wide), jnp.float32),
        ],
        compiler_params=pltpu.CompilerParams(vmem_limit_bytes=48 * 2**20),
    )(
        jnp.stack([slab, sub, rep]).astype(jnp.int32),
        wavelet,
        jnp.stack([source_z, source_y, source_x]),
        replica_seeds,
        jnp.stack([receiver_z, receiver_y, receiver_x]),
        jnp.asarray(rows_op),
        jnp.asarray(wide_op),
        blocks,
    )
    return incident_final, scattered_final, traces.reshape(STEPS, replicas, receivers)


def solution(mesh):
    slabs, subs, reps = (mesh.shape[axis] for axis in ("slab", "sub", "rep"))

    def step(courant, *rest):
        deep, tall, _ = courant.shape
        paired = all(size & (size - 1) == 0 for size in (slabs, subs, reps))
        part_width = courant.shape[2] // reps
        fits = deep * tall <= GRID_ROWS and part_width % 128 == 0
        return jax.shard_map(
            whole_shards if paired and fits else halo_shards,
            mesh=mesh,
            in_specs=(
                P("slab", "sub", None),
                P(("shot", "slab"), "sub", "rep"),
                P(("shot", "slab"), "sub", "rep"),
                P(),
                P("shot"),
                P("shot"),
                P("shot"),
                P("rep"),
                P(),
                P(),
                P(),
            ),
            out_specs=(
                P(("shot", "slab"), "sub", "rep"),
                P("rep", ("shot", "slab"), "sub", None),
                P("shot", "rep", None),
            ),
            check_vma=False,
        )(courant, *rest)

    return step
```

```python
import functools

import jax
import jax.numpy as jnp
import numpy as np
from jax import lax
from jax.experimental import pallas as pl
from jax.experimental.pallas import tpu as pltpu
from jax.sharding import PartitionSpec as P

STEPS = 4
GRID_ROWS = 512


stencil_coeffs = (-205.0 / 72.0, 8.0 / 5.0, -1.0 / 5.0, 8.0 / 315.0, -1.0 / 560.0)
pert_scale = 0.2
whole_coeffs = (-14350, 8064, -1008, 128, -9)
coeff_scale = 5040.0


def padded_2(array, sides, width):
    for axis, dim in sides:
        size, length = (lax.axis_size(axis), array.shape[dim])
        up = [(i, (i + 1) % size) for i in range(size - 1)]
        down = [(j, i) for i, j in up]
        last = lax.slice_in_dim(array, length - width, length, axis=dim)
        first = lax.slice_in_dim(array, 0, width, axis=dim)
        before = lax.ppermute(last, axis, up)
        after = lax.ppermute(first, axis, down)
        array = jnp.concatenate([before, array, after], axis=dim)
    return array


def laplace(padded):
    deep_count = padded.shape[-3] - 8
    tall_count = padded.shape[-2] - 8
    wide_count = padded.shape[-1] - 8

    def window(shift_z, shift_y, shift_x):
        return padded[
            ...,
            4 + shift_z : 4 + shift_z + deep_count,
            4 + shift_y : 4 + shift_y + tall_count,
            4 + shift_x : 4 + shift_x + wide_count,
        ]

    summed = 3.0 * stencil_coeffs[0] * window(0, 0, 0)
    for offset in range(1, 5):
        couple = (
            window(offset, 0, 0)
            + window(-offset, 0, 0)
            + window(0, offset, 0)
            + window(0, -offset, 0)
            + window(0, 0, offset)
            + window(0, 0, -offset)
        )
        summed = summed + stencil_coeffs[offset] * couple
    return summed


def perturbation(seed_values, depth_coord, height_coord, width_coord):
    hashed = (
        seed_values[:, None, None, None] * 668265263
        + depth_coord[None, :, None, None] * 73856093
        + height_coord[None, None, :, None] * 19349663
        + width_coord[None, None, None, :] * 83492791
    )
    hashed = jnp.bitwise_xor(hashed, jnp.right_shift(hashed, 15))
    hashed = hashed * 1274126177
    hashed = jnp.bitwise_xor(hashed, jnp.right_shift(hashed, 13))
    fraction = jnp.bitwise_and(hashed, 65535).astype(jnp.float32) / 65535.0
    return pert_scale * (2.0 * fraction - 1.0)


def inject(field, amounts, where_z, where_y, where_x, start_z, start_y, start_x):
    local_z = where_z - start_z
    local_y = where_y - start_y
    local_x = where_x - start_x
    inside = (
        (local_z >= 0)
        & (local_z < field.shape[0])
        & (local_y >= 0)
        & (local_y < field.shape[1])
        & (local_x >= 0)
        & (local_x < field.shape[2])
    )
    clip_z = jnp.clip(local_z, 0, field.shape[0] - 1)
    clip_y = jnp.clip(local_y, 0, field.shape[1] - 1)
    clip_x = jnp.clip(local_x, 0, field.shape[2] - 1)
    return field.at[clip_z, clip_y, clip_x].add(jnp.where(inside, amounts, jnp.zeros_like(amounts)))


def sample(field, where_z, where_y, where_x, start_z, start_y):
    local_z = where_z - start_z
    local_y = where_y - start_y
    inside = (
        (local_z >= 0) & (local_z < field.shape[1]) & (local_y >= 0) & (local_y < field.shape[2])
    )
    clip_z = jnp.clip(local_z, 0, field.shape[1] - 1)
    clip_y = jnp.clip(local_y, 0, field.shape[2] - 1)
    picked = field[:, clip_z, clip_y, where_x]
    return jnp.where(inside[None, :], picked, jnp.zeros_like(picked))


def halo_shards(
    courant,
    incident_prev,
    incident_now,
    wavelet,
    source_z,
    source_y,
    source_x,
    replica_seeds,
    receiver_z,
    receiver_y,
    receiver_x,
):
    deep_count, tall_count, part_width = incident_now.shape
    full_width = courant.shape[2]
    start_z = lax.axis_index("slab") * deep_count
    start_y = lax.axis_index("sub") * tall_count
    start_x = lax.axis_index("rep") * part_width
    speed_square = courant * courant
    depth_coord = start_z + jnp.arange(deep_count, dtype=jnp.int32)
    height_coord = start_y + jnp.arange(tall_count, dtype=jnp.int32)
    width_coord = jnp.arange(full_width, dtype=jnp.int32)
    contrast = perturbation(replica_seeds, depth_coord, height_coord, width_coord)
    whole_prev, whole_now = (
        lax.all_gather(incident_prev, "rep", axis=2, tiled=True),
        lax.all_gather(incident_now, "rep", axis=2, tiled=True),
    )
    wave_prev = jnp.zeros(contrast.shape, jnp.float32)
    wave_now = jnp.zeros(contrast.shape, jnp.float32)
    recorded = []
    for step_index in range(STEPS):
        padded = padded_2(whole_now, (("slab", 0), ("sub", 1)), 4)
        padded = jnp.pad(padded, ((0, 0), (0, 0), (4, 4)))
        whole_next = 2.0 * whole_now - whole_prev + speed_square * laplace(padded)
        whole_next = inject(
            whole_next, wavelet[step_index], source_z, source_y, source_x, start_z, start_y, 0
        )
        wave_padded = padded_2(wave_now, (("slab", 1), ("sub", 2)), 4)
        wave_padded = jnp.pad(wave_padded, ((0, 0), (0, 0), (0, 0), (4, 4)))
        source_term = 2.0 * contrast * (whole_next - 2.0 * whole_now + whole_prev)
        whole_prev, whole_now = (whole_now, whole_next)
        wave_next = 2.0 * wave_now - wave_prev + speed_square * laplace(wave_padded) + source_term
        picked = sample(wave_next, receiver_z, receiver_y, receiver_x, start_z, start_y)
        picked = lax.psum(picked, ("slab", "sub"))
        recorded.append(picked)
        wave_prev, wave_now = (wave_now, wave_next)
    traces = jnp.stack(recorded)
    incident_final = lax.dynamic_slice_in_dim(whole_now, start_x, part_width, 2)
    return (incident_final, wave_now, traces)


def band(apart):
    value = jnp.zeros(apart.shape, jnp.float32)
    for k in range(1, 5):
        value = jnp.where(apart == k, float(whole_coeffs[k]), value)
    return value


def split3(value):
    high = value.astype(jnp.bfloat16)
    rest = value - high.astype(jnp.float32)
    middle = rest.astype(jnp.bfloat16)
    low = (rest - middle.astype(jnp.float32)).astype(jnp.bfloat16)
    return high, middle, low


def product(left, right):
    return jnp.dot(left, right, preferred_element_type=jnp.float32)


def across(row, column, tall):
    far_z = jnp.abs(lax.div(row, tall) - lax.div(column, tall))
    far_y = jnp.abs(lax.rem(row, tall) - lax.rem(column, tall))
    return band(jnp.where(far_y == 0, far_z, jnp.where(far_z == 0, far_y, 0)))


def seam(value, tall, run):
    planes = value.shape[0] // tall
    sums = {}
    for z in range(planes):
        for k in range(1, 5):
            for other in (z - k, z + k):
                if 0 <= other < planes and other // run != z // run:
                    term = float(whole_coeffs[k]) * value[other * tall : (other + 1) * tall]
                    sums[z] = sums[z] + term if z in sums else term
    return sums


def doubled_contrast(cell, seed):
    hashed = cell + seed * 668265263
    hashed = hashed ^ (hashed >> 15)
    hashed = hashed * 1274126177
    hashed = hashed ^ (hashed >> 13)
    fraction = (hashed & 65535).astype(jnp.float32) / 65535.0
    return 2.0 * (pert_scale * (2.0 * fraction - 1.0))


def fetched(sources, targets, semaphores):
    copies = [
        pltpu.make_async_copy(source, target, semaphores.at[i])
        for i, (source, target) in enumerate(zip(sources, targets, strict=True))
    ]
    for copy in copies:
        copy.start()
    return copies


def pack_kernel(now_ref, prev_ref, courant_ref, own_ref, semaphores):
    layers, _, part_width = now_ref.shape
    rep = lax.axis_index("rep")
    sources = [now_ref, prev_ref]
    for x in range(2):
        at_x = pl.multiple_of((rep ^ x) * part_width, part_width)
        sources.append(courant_ref.at[:, :, pl.ds(at_x, part_width)])
    targets = [own_ref.at[pl.ds(i * layers, layers)] for i in range(4)]
    for copy in fetched(sources, targets, semaphores):
        copy.wait()


def prepare_kernel(own_shape, *refs):
    place_ref, refs = refs[0], refs[1:]
    given, outputs, held, semaphores = refs[:8], refs[8:16], refs[16:24], refs[24]
    contrast_ref, force_ref, last_contrast_ref, last_force_ref = outputs[:4]
    rows_ref, wide_ref, last_ref, mask_ref = outputs[4:]
    wavelet_ref, source_z_ref, source_y_ref, source_x_ref = held[:4]
    seeds_ref, receiver_z_ref, receiver_y_ref, receiver_x_ref = held[4:]
    copies = fetched(given, held, semaphores)
    deep, tall, wide = force_ref.shape[1:]
    rows = deep * tall
    runs, tops, block = rows_ref.shape[0], rows_ref.shape[1], rows_ref.shape[2] // 3
    receivers = mask_ref.shape[0]
    deep_count, tall_count = own_shape
    own = deep_count * tall_count
    replicas = seeds_ref.shape[0]
    sources = range(source_z_ref.shape[0])
    line = lax.broadcasted_iota(jnp.int32, (wide, wide), 0)
    beside = band(jnp.abs(line - lax.broadcasted_iota(jnp.int32, (wide, wide), 1)))
    for part in range(3):
        wide_ref[part * wide : (part + 1) * wide, :] = beside.astype(jnp.bfloat16)
    for copy in copies:
        copy.wait()
    z_of = lax.broadcasted_iota(jnp.int32, (deep, tall, wide), 0)
    y_of = lax.broadcasted_iota(jnp.int32, (deep, tall, wide), 1)
    x_of = lax.broadcasted_iota(jnp.int32, (deep, tall, wide), 2)
    cell = z_of * 73856093 + y_of * 19349663 + x_of * 83492791
    for r in range(replicas):
        contrast_ref[r] = doubled_contrast(cell, seeds_ref[r])
    lane = lax.broadcasted_iota(jnp.int32, (1, wide), 1)
    force_ref[...] = jnp.zeros_like(force_ref)
    for n in range(STEPS - 1):
        for k in sources:
            at = (n, source_z_ref[k], pl.ds(source_y_ref[k], 1), slice(None))
            force_ref[at] += jnp.where(lane == source_x_ref[k], wavelet_ref[n, k], 0.0)
    index = lax.broadcasted_iota(jnp.int32, (own + receivers, 1), 0)
    row = (place_ref[0] * deep_count + lax.div(index, tall_count)) * tall
    row += place_ref[1] * tall_count + lax.rem(index, tall_count)
    for j in range(receivers):
        row = jnp.where(index == own + j, receiver_z_ref[j] * tall + receiver_y_ref[j], row)
        mask_ref[pl.ds(j, 1), :] = jnp.where(lane == receiver_x_ref[j], 1.0, 0.0)
    cell = lax.div(row, tall) * 73856093 + lax.rem(row, tall) * 19349663 + lane * 83492791
    for r in range(replicas):
        last_contrast_ref[r] = doubled_contrast(cell, seeds_ref[r])
    force = jnp.zeros((own + receivers, wide), jnp.float32)
    for k in sources:
        here = (row == source_z_ref[k] * tall + source_y_ref[k]) & (lane == source_x_ref[k])
        force += jnp.where(here, wavelet_ref[STEPS - 1, k], 0.0)
    last_force_ref[...] = force
    column = lax.broadcasted_iota(jnp.int32, (1, rows), 1)
    taken = jnp.where(row[own:] == column, 1.0, 0.0)
    last = jnp.concatenate([across(row, column, tall), taken], axis=0).astype(jnp.bfloat16)
    line = lax.broadcasted_iota(jnp.int32, (block, 1), 0)
    inner = across(line, column[:, :block], tall).astype(jnp.bfloat16)
    for part in range(3):
        last_ref[:, part * rows : (part + 1) * rows] = last
        for run in range(runs):
            here = (run, slice(0, block), slice(part * block, (part + 1) * block))
            rows_ref[here] = inner
            here = (run, slice(block, tops), slice(part * block, (part + 1) * block))
            rows_ref[here] = taken[:, run * block : (run + 1) * block].astype(jnp.bfloat16)


def step_kernel(
    layout,
    own_shape,
    place_ref,
    contrast_ref,
    force_ref,
    last_contrast_ref,
    last_force_ref,
    rows_ref,
    wide_ref,
    last_ref,
    mask_ref,
    *refs,
):
    blocks, refs = refs[:-8], refs[-8:]
    incident_ref, scattered_ref, traces_ref, field_ref, speed_ref, drive_ref, wave_ref, slim_ref = refs
    deep, tall, wide = speed_ref.shape
    rows = deep * tall
    shape, cube = (rows, wide), (deep, tall, wide)
    deep_count, tall_count, part_width = own_shape
    own = deep_count * tall_count
    replicas = contrast_ref.shape[0]
    receivers = mask_ref.shape[0]
    runs, block = rows_ref.shape[0], rows_ref.shape[2] // 3
    run = block // tall
    slab, sub, rep = place_ref[0], place_ref[1], place_ref[2]

    for number, layer, what, x, y, z in layout:
        at = (
            pl.ds(pl.multiple_of((slab ^ z) * deep_count, deep_count), deep_count),
            pl.ds(pl.multiple_of((sub ^ y) * tall_count, tall_count), tall_count),
        )
        at += (pl.ds(pl.multiple_of((rep ^ x) * part_width, part_width), part_width),)
        piece = blocks[number][layer : layer + deep_count]
        if what == "courant":
            speed_ref[at] = piece * piece * (1.0 / coeff_scale)
        else:
            field_ref[(("now", "prev").index(what),) + at] = piece

    def applied(value):
        parts = split3(value)
        total = (3.0 * whole_coeffs[0]) * value
        total += product(jnp.concatenate(parts, axis=1), wide_ref[...])
        down, taken = [], None
        for number in range(runs):
            here = slice(number * block, (number + 1) * block)
            result = product(rows_ref[number], jnp.concatenate([part[here] for part in parts], axis=0))
            down.append(result[:block])
            taken = result[block:] if taken is None else taken + result[block:]
        total += jnp.concatenate(down, axis=0)
        sums = seam(value, tall, run)
        pieces = []
        for z in range(deep):
            piece = total[z * tall : (z + 1) * tall]
            pieces.append(piece + sums[z] if z in sums else piece)
        return jnp.concatenate(pieces, axis=0), taken

    def flat(ref, *index):
        return ref[index].reshape(shape)

    at_z = pl.multiple_of(slab * deep_count, deep_count)
    at_y = pl.multiple_of(sub * tall_count, tall_count)
    at_x = pl.multiple_of(rep * part_width, part_width)

    def owned(ref, *index):
        here = index + (pl.ds(at_z, deep_count), pl.ds(at_y, tall_count), slice(None))
        return ref[here].reshape(own, wide)

    samples = [[None] * replicas for _ in range(STEPS)]
    speed = flat(speed_ref)

    now = flat(field_ref, 0)
    drive_ref[...] = speed * applied(now)[0] + flat(force_ref, 0)
    field_ref[1] = (2.0 * now - flat(field_ref, 1) + drive_ref[...]).reshape(cube)
    for r in range(replicas):
        wave = flat(contrast_ref, r) * drive_ref[...]
        wave_ref[0, r] = wave.reshape(cube)
        result, samples[0][r] = applied(wave)
        wave_ref[1, r] = (2.0 * wave + speed * result).reshape(cube)

    now = flat(field_ref, 1)
    drive_ref[...] = speed * applied(now)[0] + flat(force_ref, 1)
    field_ref[0] = (2.0 * now - flat(field_ref, 0) + drive_ref[...]).reshape(cube)
    for r in range(replicas):
        wave_ref[1, r] += (flat(contrast_ref, r) * drive_ref[...]).reshape(cube)

    now = flat(field_ref, 0)
    drive_ref[...] = speed * applied(now)[0] + flat(force_ref, 2)
    field_ref[1] = (2.0 * now - flat(field_ref, 1) + drive_ref[...]).reshape(cube)
    for r in range(replicas):
        wave = flat(wave_ref, 1, r)
        result, samples[1][r] = applied(wave)
        source = flat(contrast_ref, r) * drive_ref[...]
        wave_ref[0, r] = (
            2.0 * wave - flat(wave_ref, 0, r) + speed * result + source
        ).reshape(cube)

    taken = product(last_ref[own + receivers :], jnp.concatenate(split3(speed), axis=0))
    speed = jnp.concatenate([owned(speed_ref), taken], axis=0)

    def last_applied(value, mine):
        result = product(last_ref[...], jnp.concatenate(split3(value), axis=0))
        here = jnp.concatenate([mine, result[own + receivers :]], axis=0)
        total = (3.0 * whole_coeffs[0]) * here + result[: own + receivers]
        return total + product(jnp.concatenate(split3(here), axis=1), wide_ref[...]), here

    result, now = last_applied(flat(field_ref, 1), owned(field_ref, 1))
    drive = speed * result + last_force_ref[...]
    slim_ref[...] = 2.0 * now[:own] - owned(field_ref, 0) + drive[:own]
    incident_ref[...] = slim_ref[:, pl.ds(at_x, part_width)].reshape(incident_ref.shape)
    for r in range(replicas):
        result, wave = last_applied(flat(wave_ref, 0, r), owned(wave_ref, 0, r))
        samples[2][r] = wave[own:]
        before = jnp.concatenate([owned(wave_ref, 1, r), samples[1][r]], axis=0)
        following = 2.0 * wave - before + speed * result + last_contrast_ref[r] * drive
        scattered_ref[r] = following[:own].reshape(scattered_ref.shape[1:])
        samples[3][r] = following[own:]
    column = lax.broadcasted_iota(jnp.int32, (receivers, 128), 1)
    gathered = jnp.zeros((receivers, 128), jnp.float32)
    mask = mask_ref[...]
    for n in range(STEPS):
        for r in range(replicas):
            summed = jnp.sum(samples[n][r] * mask, axis=1, keepdims=True)
            gathered += jnp.where(column == n * replicas + r, summed, 0.0)
    traces_ref[...] = jnp.transpose(gathered)[: STEPS * replicas, :]


def swapped(array, axis, distance):
    size = lax.axis_size(axis)
    return lax.ppermute(array, axis, [(i, i ^ distance) for i in range(size)])


def exchanged(own, deep_count, prepared):
    sent = own[: 3 * deep_count]
    beyond = {m: swapped(sent, "slab", m) for m in (1, 2, 3)}
    near = jnp.concatenate([own[: 2 * deep_count], beyond[1]], axis=0)
    far = jnp.concatenate([beyond[2], beyond[3]], axis=0)
    far, prepared = lax.optimization_barrier((far, prepared))
    near_two, far_two = swapped(near, "rep", 1), swapped(far, "rep", 1)
    near_line = jnp.concatenate([near, near_two, own[2 * deep_count :]], axis=0)
    blocks = [near_line, far, far_two]
    blocks += [swapped(block, "sub", 1) for block in blocks]
    names = ("now", "prev", "courant")
    near_layout = [(name, 0) for name in names[:2]] + [(name, 1) for name in names]
    near_layout = [(name, x, z) for x in range(2) for name, z in near_layout]
    near_layout += [("courant", x, 0) for x in range(2)]
    far_layout = [(name, m) for m in (2, 3) for name in names]
    layout = []
    for y in range(2):
        for i, (name, x, z) in enumerate(near_layout):
            layout.append((3 * y, i * deep_count, name, x, y, z))
        for x in range(2):
            for i, (name, z) in enumerate(far_layout):
                layout.append((3 * y + 1 + x, i * deep_count, name, x, y, z))
    return blocks, tuple(layout), prepared


def whole_shards(
    courant,
    incident_prev,
    incident_now,
    wavelet,
    source_z,
    source_y,
    source_x,
    replica_seeds,
    receiver_z,
    receiver_y,
    receiver_x,
):
    deep_count, tall_count, part_width = incident_now.shape
    wide = courant.shape[2]
    slab, sub, rep = (lax.axis_index(axis) for axis in ("slab", "sub", "rep"))
    deep, tall = lax.axis_size("slab") * deep_count, lax.axis_size("sub") * tall_count
    rows = deep * tall
    replicas, receivers = replica_seeds.shape[0], receiver_z.shape[0]
    own_shape = (deep_count, tall_count, part_width)
    cube = (deep, tall, wide)
    last_rows = deep_count * tall_count + receivers
    block = min(rows, 256)
    smem = pl.BlockSpec(memory_space=pltpu.SMEM)
    vmem = pl.BlockSpec(memory_space=pltpu.VMEM)
    anywhere = pl.BlockSpec(memory_space=pltpu.HBM)

    def held(*shape, dtype=jnp.float32):
        return jax.ShapeDtypeStruct(shape, dtype)

    def call(kernel, out_shape, scalars, distant, arrays, scratch):
        return pl.pallas_call(
            kernel,
            out_shape=out_shape,
            in_specs=[smem] * len(scalars) + [anywhere] * len(distant) + [vmem] * len(arrays),
            out_specs=tuple(vmem for _ in out_shape),
            scratch_shapes=list(scratch),
            compiler_params=pltpu.CompilerParams(vmem_limit_bytes=24 * 2**20),
        )(*scalars, *(pltpu.with_memory_space_constraint(a, pltpu.HBM) for a in distant), *arrays)

    place = jnp.stack([slab, sub, rep]).astype(jnp.int32)
    given = (
        wavelet,
        source_z,
        source_y,
        source_x,
        replica_seeds,
        receiver_z,
        receiver_y,
        receiver_x,
    )
    prepared = call(
        functools.partial(prepare_kernel, own_shape[:2]),
        (
            held(replicas, *cube),
            held(STEPS - 1, *cube),
            held(replicas, last_rows, wide),
            held(last_rows, wide),
            held(rows // block, block + receivers, 3 * block, dtype=jnp.bfloat16),
            held(3 * wide, wide, dtype=jnp.bfloat16),
            held(last_rows + receivers, 3 * rows, dtype=jnp.bfloat16),
            held(receivers, wide),
        ),
        (place,),
        given,
        (),
        (
            *(pltpu.SMEM(array.shape, array.dtype) for array in given),
            pltpu.SemaphoreType.DMA((len(given),)),
        ),
    )
    own = call(
        pack_kernel,
        (held(4 * deep_count, tall_count, part_width),),
        (),
        (incident_now, incident_prev, courant),
        (),
        (pltpu.SemaphoreType.DMA((4,)),),
    )[0]
    blocks, layout, prepared = exchanged(own, deep_count, prepared)
    incident_final, scattered_final, traces = call(
        functools.partial(step_kernel, layout, own_shape),
        (
            held(*own_shape),
            held(replicas, deep_count, tall_count, wide),
            held(STEPS * replicas, receivers),
        ),
        (place,),
        (),
        (*prepared, *blocks),
        (
            pltpu.VMEM((2,) + cube, jnp.float32),
            pltpu.VMEM(cube, jnp.float32),
            pltpu.VMEM((rows, wide), jnp.float32),
            pltpu.VMEM((2, replicas) + cube, jnp.float32),
            pltpu.VMEM((deep_count * tall_count, wide), jnp.float32),
        ),
    )
    return incident_final, scattered_final, traces.reshape(STEPS, replicas, receivers)


def solution(mesh):
    slabs, subs, reps = (mesh.shape[axis] for axis in ("slab", "sub", "rep"))

    def step(courant, *rest):
        deep, tall, _ = courant.shape
        paired = (slabs, subs, reps, mesh.shape["shot"]) == (4, 2, 2, 2)
        part_width = courant.shape[2] // reps
        fits = deep * tall <= GRID_ROWS and part_width % 128 == 0
        return jax.shard_map(
            whole_shards if paired and fits else halo_shards,
            mesh=mesh,
            in_specs=(
                P("slab", "sub", None),
                P(("shot", "slab"), "sub", "rep"),
                P(("shot", "slab"), "sub", "rep"),
                P(),
                P("shot"),
                P("shot"),
                P("shot"),
                P("rep"),
                P(),
                P(),
                P(),
            ),
            out_specs=(
                P(("shot", "slab"), "sub", "rep"),
                P("rep", ("shot", "slab"), "sub", None),
                P("shot", "rep", None),
            ),
            check_vma=False,
        )(courant, *rest)

    return step
```

```python
import functools

import jax
import jax.numpy as jnp
import numpy as np
from jax import lax
from jax.experimental import pallas as pl
from jax.experimental.pallas import tpu as pltpu
from jax.sharding import PartitionSpec as P

STEPS = 4
GRID_ROWS = 512
CHUNK = 2
WAVE_PARTS = 2


stencil_coeffs = (-205.0 / 72.0, 8.0 / 5.0, -1.0 / 5.0, 8.0 / 315.0, -1.0 / 560.0)
pert_scale = 0.2
whole_coeffs = (-14350, 8064, -1008, 128, -9)
coeff_scale = 5040.0


def padded_2(array, sides, width):
    for axis, dim in sides:
        size, length = (lax.axis_size(axis), array.shape[dim])
        up = [(i, (i + 1) % size) for i in range(size - 1)]
        down = [(j, i) for i, j in up]
        last = lax.slice_in_dim(array, length - width, length, axis=dim)
        first = lax.slice_in_dim(array, 0, width, axis=dim)
        before = lax.ppermute(last, axis, up)
        after = lax.ppermute(first, axis, down)
        array = jnp.concatenate([before, array, after], axis=dim)
    return array


def laplace(padded):
    deep_count = padded.shape[-3] - 8
    tall_count = padded.shape[-2] - 8
    wide_count = padded.shape[-1] - 8

    def window(shift_z, shift_y, shift_x):
        return padded[
            ...,
            4 + shift_z : 4 + shift_z + deep_count,
            4 + shift_y : 4 + shift_y + tall_count,
            4 + shift_x : 4 + shift_x + wide_count,
        ]

    summed = 3.0 * stencil_coeffs[0] * window(0, 0, 0)
    for offset in range(1, 5):
        couple = (
            window(offset, 0, 0)
            + window(-offset, 0, 0)
            + window(0, offset, 0)
            + window(0, -offset, 0)
            + window(0, 0, offset)
            + window(0, 0, -offset)
        )
        summed = summed + stencil_coeffs[offset] * couple
    return summed


def perturbation(seed_values, depth_coord, height_coord, width_coord):
    hashed = (
        seed_values[:, None, None, None] * 668265263
        + depth_coord[None, :, None, None] * 73856093
        + height_coord[None, None, :, None] * 19349663
        + width_coord[None, None, None, :] * 83492791
    )
    hashed = jnp.bitwise_xor(hashed, jnp.right_shift(hashed, 15))
    hashed = hashed * 1274126177
    hashed = jnp.bitwise_xor(hashed, jnp.right_shift(hashed, 13))
    fraction = jnp.bitwise_and(hashed, 65535).astype(jnp.float32) / 65535.0
    return pert_scale * (2.0 * fraction - 1.0)


def inject(field, amounts, where_z, where_y, where_x, start_z, start_y, start_x):
    local_z = where_z - start_z
    local_y = where_y - start_y
    local_x = where_x - start_x
    inside = (
        (local_z >= 0)
        & (local_z < field.shape[0])
        & (local_y >= 0)
        & (local_y < field.shape[1])
        & (local_x >= 0)
        & (local_x < field.shape[2])
    )
    clip_z = jnp.clip(local_z, 0, field.shape[0] - 1)
    clip_y = jnp.clip(local_y, 0, field.shape[1] - 1)
    clip_x = jnp.clip(local_x, 0, field.shape[2] - 1)
    return field.at[clip_z, clip_y, clip_x].add(jnp.where(inside, amounts, jnp.zeros_like(amounts)))


def sample(field, where_z, where_y, where_x, start_z, start_y):
    local_z = where_z - start_z
    local_y = where_y - start_y
    inside = (
        (local_z >= 0) & (local_z < field.shape[1]) & (local_y >= 0) & (local_y < field.shape[2])
    )
    clip_z = jnp.clip(local_z, 0, field.shape[1] - 1)
    clip_y = jnp.clip(local_y, 0, field.shape[2] - 1)
    picked = field[:, clip_z, clip_y, where_x]
    return jnp.where(inside[None, :], picked, jnp.zeros_like(picked))


def halo_shards(
    courant,
    incident_prev,
    incident_now,
    wavelet,
    source_z,
    source_y,
    source_x,
    replica_seeds,
    receiver_z,
    receiver_y,
    receiver_x,
):
    deep_count, tall_count, part_width = incident_now.shape
    full_width = courant.shape[2]
    start_z = lax.axis_index("slab") * deep_count
    start_y = lax.axis_index("sub") * tall_count
    start_x = lax.axis_index("rep") * part_width
    speed_square = courant * courant
    depth_coord = start_z + jnp.arange(deep_count, dtype=jnp.int32)
    height_coord = start_y + jnp.arange(tall_count, dtype=jnp.int32)
    width_coord = jnp.arange(full_width, dtype=jnp.int32)
    contrast = perturbation(replica_seeds, depth_coord, height_coord, width_coord)
    whole_prev, whole_now = (
        lax.all_gather(incident_prev, "rep", axis=2, tiled=True),
        lax.all_gather(incident_now, "rep", axis=2, tiled=True),
    )
    wave_prev = jnp.zeros(contrast.shape, jnp.float32)
    wave_now = jnp.zeros(contrast.shape, jnp.float32)
    recorded = []
    for step_index in range(STEPS):
        padded = padded_2(whole_now, (("slab", 0), ("sub", 1)), 4)
        padded = jnp.pad(padded, ((0, 0), (0, 0), (4, 4)))
        whole_next = 2.0 * whole_now - whole_prev + speed_square * laplace(padded)
        whole_next = inject(
            whole_next, wavelet[step_index], source_z, source_y, source_x, start_z, start_y, 0
        )
        wave_padded = padded_2(wave_now, (("slab", 1), ("sub", 2)), 4)
        wave_padded = jnp.pad(wave_padded, ((0, 0), (0, 0), (0, 0), (4, 4)))
        source_term = 2.0 * contrast * (whole_next - 2.0 * whole_now + whole_prev)
        whole_prev, whole_now = (whole_now, whole_next)
        wave_next = 2.0 * wave_now - wave_prev + speed_square * laplace(wave_padded) + source_term
        picked = sample(wave_next, receiver_z, receiver_y, receiver_x, start_z, start_y)
        picked = lax.psum(picked, ("slab", "sub"))
        recorded.append(picked)
        wave_prev, wave_now = (wave_now, wave_next)
    traces = jnp.stack(recorded)
    incident_final = lax.dynamic_slice_in_dim(whole_now, start_x, part_width, 2)
    return (incident_final, wave_now, traces)


def band(apart):
    value = jnp.zeros(apart.shape, jnp.float32)
    for k in range(1, 5):
        value = jnp.where(apart == k, float(whole_coeffs[k]), value)
    return value


def split(value, count):
    parts = []
    for part in range(count):
        parts.append(value.astype(jnp.bfloat16))
        if part < count - 1:
            value = value - parts[-1].astype(jnp.float32)
    return parts


def product(left, right):
    return jnp.dot(left, right, preferred_element_type=jnp.float32)


def across(row, column, tall):
    far_z = jnp.abs(lax.div(row, tall) - lax.div(column, tall))
    far_y = jnp.abs(lax.rem(row, tall) - lax.rem(column, tall))
    return band(jnp.where(far_y == 0, far_z, jnp.where(far_z == 0, far_y, 0)))


def doubled_contrast(cell, seed):
    hashed = cell + seed * 668265263
    hashed = hashed ^ (hashed >> 15)
    hashed = hashed * 1274126177
    hashed = hashed ^ (hashed >> 13)
    fraction = (hashed & 65535).astype(jnp.float32) / 65535.0
    return 2.0 * (pert_scale * (2.0 * fraction - 1.0))


def fetched(sources, targets, semaphores):
    copies = [
        pltpu.make_async_copy(source, target, semaphores.at[i])
        for i, (source, target) in enumerate(zip(sources, targets, strict=True))
    ]
    for copy in copies:
        copy.start()
    return copies


def pack_kernel(now_ref, prev_ref, courant_ref, own_ref, semaphores):
    layers, _, part_width = now_ref.shape
    rep = lax.axis_index("rep")
    sources = [now_ref, prev_ref]
    for x in range(2):
        at_x = pl.multiple_of((rep ^ x) * part_width, part_width)
        sources.append(courant_ref.at[:, :, pl.ds(at_x, part_width)])
    targets = [own_ref.at[pl.ds(i * layers, layers)] for i in range(4)]
    for copy in fetched(sources, targets, semaphores):
        copy.wait()


def prepare_kernel(own_shape, *refs):
    place_ref, refs = refs[0], refs[1:]
    given, outputs, held, semaphores = refs[:8], refs[8:16], refs[16:24], refs[24]
    contrast_ref, force_ref, last_contrast_ref, last_force_ref = outputs[:4]
    rows_ref, wide_ref, last_ref, mask_ref = outputs[4:]
    wavelet_ref, source_z_ref, source_y_ref, source_x_ref = held[:4]
    seeds_ref, receiver_z_ref, receiver_y_ref, receiver_x_ref = held[4:]
    copies = fetched(given, held, semaphores)
    deep, tall, wide = force_ref.shape[1:]
    rows = deep * tall
    runs, tops, block = rows_ref.shape[0], rows_ref.shape[1], rows_ref.shape[2] // 3
    receivers = mask_ref.shape[0]
    deep_count, tall_count = own_shape
    own = deep_count * tall_count
    replicas = seeds_ref.shape[0]
    sources = range(source_z_ref.shape[0])
    line = lax.broadcasted_iota(jnp.int32, (wide, wide), 0)
    beside = band(jnp.abs(line - lax.broadcasted_iota(jnp.int32, (wide, wide), 1)))
    for part in range(3):
        wide_ref[part * wide : (part + 1) * wide, :] = beside.astype(jnp.bfloat16)
    for copy in copies:
        copy.wait()
    z_of = lax.broadcasted_iota(jnp.int32, (deep, tall, wide), 0)
    y_of = lax.broadcasted_iota(jnp.int32, (deep, tall, wide), 1)
    x_of = lax.broadcasted_iota(jnp.int32, (deep, tall, wide), 2)
    cell = z_of * 73856093 + y_of * 19349663 + x_of * 83492791
    for r in range(replicas):
        contrast_ref[r] = doubled_contrast(cell, seeds_ref[r])
    lane = lax.broadcasted_iota(jnp.int32, (1, wide), 1)
    force_ref[...] = jnp.zeros_like(force_ref)
    for n in range(STEPS - 1):
        for k in sources:
            at = (n, source_z_ref[k], pl.ds(source_y_ref[k], 1), slice(None))
            force_ref[at] += jnp.where(lane == source_x_ref[k], wavelet_ref[n, k], 0.0)
    index = lax.broadcasted_iota(jnp.int32, (own + receivers, 1), 0)
    row = (place_ref[0] * deep_count + lax.div(index, tall_count)) * tall
    row += place_ref[1] * tall_count + lax.rem(index, tall_count)
    for j in range(receivers):
        row = jnp.where(index == own + j, receiver_z_ref[j] * tall + receiver_y_ref[j], row)
        mask_ref[pl.ds(j, 1), :] = jnp.where(lane == receiver_x_ref[j], 1.0, 0.0)
    cell = lax.div(row, tall) * 73856093 + lax.rem(row, tall) * 19349663 + lane * 83492791
    for r in range(replicas):
        last_contrast_ref[r] = doubled_contrast(cell, seeds_ref[r])
    force = jnp.zeros((own + receivers, wide), jnp.float32)
    for k in sources:
        here = (row == source_z_ref[k] * tall + source_y_ref[k]) & (lane == source_x_ref[k])
        force += jnp.where(here, wavelet_ref[STEPS - 1, k], 0.0)
    last_force_ref[...] = force
    column = lax.broadcasted_iota(jnp.int32, (1, rows), 1)
    taken = jnp.where(row[own:] == column, 1.0, 0.0)
    last = jnp.concatenate([across(row, column, tall), taken], axis=0).astype(jnp.bfloat16)
    line = lax.broadcasted_iota(jnp.int32, (block, 1), 0)
    inner = across(line, column[:, :block], tall).astype(jnp.bfloat16)
    for part in range(3):
        for run in range(runs):
            start = (3 * run + part) * block
            last_ref[:, start : start + block] = last[:, run * block : (run + 1) * block]
            here = (run, slice(0, block), slice(part * block, (part + 1) * block))
            rows_ref[here] = inner
            here = (run, slice(block, tops), slice(part * block, (part + 1) * block))
            rows_ref[here] = taken[:, run * block : (run + 1) * block].astype(jnp.bfloat16)


def step_kernel(
    layout,
    own_shape,
    place_ref,
    contrast_ref,
    force_ref,
    last_contrast_ref,
    last_force_ref,
    rows_ref,
    wide_ref,
    last_ref,
    mask_ref,
    *refs,
):
    blocks, refs = refs[:-11], refs[-11:]
    incident_ref, scattered_ref, traces_ref = refs[:3]
    field_ref, speed_ref, drive_ref, wave_ref, parts_ref, product_ref, taken_ref, slim_ref = refs[3:]
    deep, tall, wide = speed_ref.shape
    deep_count, tall_count, part_width = own_shape
    own = deep_count * tall_count
    replicas = contrast_ref.shape[0]
    receivers = mask_ref.shape[0]
    runs, block = rows_ref.shape[0], rows_ref.shape[2] // 3
    run = block // tall
    group = min(run, CHUNK)
    slab, sub, rep = (place_ref[i] for i in range(3))

    for number, layer, what, x, y, z in layout:
        half = rep ^ x
        at = (
            pl.ds(pl.multiple_of((slab ^ z) * deep_count, deep_count), deep_count),
            pl.ds(pl.multiple_of((sub ^ y) * tall_count, tall_count), tall_count),
            pl.ds(pl.multiple_of(half * part_width, part_width), part_width),
        )
        piece = blocks[number][layer : layer + deep_count]
        if what == "courant":
            speed_ref[at] = piece * piece * (1.0 / coeff_scale)
        else:
            field_ref[(("prev", "now").index(what),) + at] = piece

    def groups(number):
        for first in range(number * run, (number + 1) * run, group):
            yield first, slice((first - number * run) * tall, (first - number * run + group) * tall)

    def flat(ref, *index):
        value = ref[index]
        return value.reshape(-1, wide)

    def near(ref, first, *index):
        return flat(ref, *index, slice(first, first + group))

    def put(ref, value, first, *index):
        ref[index + (slice(first, first + group),)] = value.reshape(group, tall, wide)

    def cut(slot, number, rows, value, count):
        for part, piece in enumerate(split(value, count)):
            parts_ref[slot, number, part * block + rows.start : part * block + rows.stop] = piece

    def multiply(slot, number, count, sampled):
        held = parts_ref[slot, number, : count * block]
        tops = rows_ref.shape[1] if sampled else block
        beside = jnp.concatenate([held[part * block : (part + 1) * block] for part in range(count)], axis=1)
        down = product(rows_ref[number, :tops, : count * block], held)
        product_ref[slot, number] = down[:block] + product(beside, wide_ref[: count * wide])
        if sampled:
            taken_ref[slot, number] = down[block:]

    def applied(slot, number, rows, first, ref, *index):
        total = (3.0 * whole_coeffs[0]) * near(ref, first, *index) + product_ref[slot, number, rows]
        pieces = []
        for z in range(first, first + group):
            piece = total[(z - first) * tall : (z - first + 1) * tall]
            for k in range(1, 5):
                for other in (z - k, z + k):
                    if 0 <= other < deep and other // run != z // run:
                        piece = piece + float(whole_coeffs[k]) * ref[index + (other,)]
            pieces.append(piece)
        return jnp.concatenate(pieces, axis=0) if len(pieces) > 1 else pieces[0]

    def start_incident(number):
        for first, rows in groups(number):
            cut(0, number, rows, near(field_ref, first, 1), 3)

    def step_incident(n, number):
        before, now, after = n % 4, (n + 1) % 4, (n + 2) % 4
        for first, rows in groups(number):
            drive = near(speed_ref, first) * applied(0, number, rows, first, field_ref, now)
            drive += near(force_ref, first, n)
            put(drive_ref, drive, first)
            following = 2.0 * near(field_ref, first, now) - near(field_ref, first, before) + drive
            put(field_ref, following, first, after)
            cut(0, number, rows, following, 3)
            if n == 0:
                for r in range(replicas):
                    wave = near(contrast_ref, first, r) * drive
                    put(wave_ref, wave, first, r, 0)
                    cut(1 + r, number, rows, wave, WAVE_PARTS)

    def step_wave(n, r, number):
        for first, rows in groups(number):
            following = (
                2.0 * near(wave_ref, first, r, n - 1)
                + near(speed_ref, first) * applied(1 + r, number, rows, first, wave_ref, r, n - 1)
                + near(contrast_ref, first, r) * near(drive_ref, first)
            )
            if n > 1:
                following -= near(wave_ref, first, r, n - 2)
            put(wave_ref, following, first, r, n)
            cut(1 + r, number, rows, following, WAVE_PARTS)

    at_z = pl.multiple_of(slab * deep_count, deep_count)
    at_y = pl.multiple_of(sub * tall_count, tall_count)
    at_x = pl.multiple_of(rep * part_width, part_width)

    def owned(ref, *index):
        here = index + (pl.ds(at_z, deep_count), pl.ds(at_y, tall_count), slice(None))
        return ref[here].reshape(own, wide)

    def chosen(slot, rows, count):
        total = None
        for number in range(runs):
            start = number * 3 * block
            held = parts_ref[slot, number, : count * block]
            term = product(last_ref[rows, start : start + count * block], held)
            total = term if total is None else total + term
        return total

    samples = [[None] * replicas for _ in range(STEPS)]
    each = range(runs)

    for number in each:
        start_incident(number)
    for number in each:
        multiply(0, number, 3, False)
    for number in each:
        for first, rows in groups(number):
            cut(1 + replicas, number, rows, near(speed_ref, first), 3)
    for number in each:
        step_incident(0, number)
    for n in (1, 2):
        work = [(multiply, (0, number, 3, False)) for number in each]
        after = [(step_incident, (n, number)) for number in each]
        for r in range(replicas):
            work += [(multiply, (1 + r, number, WAVE_PARTS, True)) for number in each]
            after += [(step_wave, (n, r, number)) for number in each]
        for i in range(len(work) + runs):
            if i < len(work):
                work[i][0](*work[i][1])
            if i >= runs:
                after[i - runs][0](*after[i - runs][1])
        for r in range(replicas):
            samples[n - 1][r] = sum(taken_ref[1 + r, number] for number in each)

    receiver_rows = slice(own + receivers, own + 2 * receivers)
    speed = jnp.concatenate([owned(speed_ref), chosen(1 + replicas, receiver_rows, 3)], axis=0)

    def last_applied(slot, mine, count):
        result = chosen(slot, slice(None), count)
        here = jnp.concatenate([mine, result[own + receivers :]], axis=0)
        total = (3.0 * whole_coeffs[0]) * here + result[: own + receivers]
        beside = jnp.concatenate(split(here, count), axis=1)
        return total + product(beside, wide_ref[: count * wide]), here

    result, now = last_applied(0, owned(field_ref, 0), 3)
    drive = speed * result + last_force_ref[...]
    slim_ref[...] = 2.0 * now[:own] - owned(field_ref, 3) + drive[:own]
    incident_ref[...] = slim_ref[:, pl.ds(at_x, part_width)].reshape(incident_ref.shape)
    for r in range(replicas):
        result, wave = last_applied(1 + r, owned(wave_ref, r, 2), WAVE_PARTS)
        samples[2][r] = wave[own:]
        before = jnp.concatenate([owned(wave_ref, r, 1), samples[1][r]], axis=0)
        following = 2.0 * wave - before + speed * result + last_contrast_ref[r] * drive
        scattered_ref[r] = following[:own].reshape(scattered_ref.shape[1:])
        samples[3][r] = following[own:]
    column = lax.broadcasted_iota(jnp.int32, (receivers, 128), 1)
    gathered = jnp.zeros((receivers, 128), jnp.float32)
    mask = mask_ref[...]
    for n in range(STEPS):
        for r in range(replicas):
            summed = jnp.sum(samples[n][r] * mask, axis=1, keepdims=True)
            gathered += jnp.where(column == n * replicas + r, summed, 0.0)
    traces_ref[...] = jnp.transpose(gathered)[: STEPS * replicas, :]


def swapped(array, axis, distance):
    size = lax.axis_size(axis)
    return lax.ppermute(array, axis, [(i, i ^ distance) for i in range(size)])


def exchanged(own, deep_count, prepared):
    sent = own[: 3 * deep_count]
    beyond = {m: swapped(sent, "slab", m) for m in (1, 2, 3)}
    near = jnp.concatenate([own[: 2 * deep_count], beyond[1]], axis=0)
    far = jnp.concatenate([beyond[3], beyond[2]], axis=0)
    far, prepared = lax.optimization_barrier((far, prepared))
    near_two, far_two = swapped(near, "rep", 1), swapped(far, "rep", 1)
    near_line = jnp.concatenate([near, near_two, own[2 * deep_count :]], axis=0)
    blocks = [near_line, far, far_two]
    blocks += [swapped(block, "sub", 1) for block in blocks]
    names = ("now", "prev", "courant")
    near_layout = [(name, 0) for name in names[:2]] + [(name, 1) for name in names]
    near_layout = [(name, x, z) for x in range(2) for name, z in near_layout]
    near_layout += [("courant", x, 0) for x in range(2)]
    far_layout = [(name, m) for m in (3, 2) for name in names]
    layout = []
    for y in range(2):
        for i, (name, x, z) in enumerate(near_layout):
            layout.append((3 * y, i * deep_count, name, x, y, z))
        for x in range(2):
            for i, (name, z) in enumerate(far_layout):
                layout.append((3 * y + 1 + x, i * deep_count, name, x, y, z))
    return blocks, tuple(layout), prepared


def whole_shards(
    courant,
    incident_prev,
    incident_now,
    wavelet,
    source_z,
    source_y,
    source_x,
    replica_seeds,
    receiver_z,
    receiver_y,
    receiver_x,
):
    deep_count, tall_count, part_width = incident_now.shape
    wide = courant.shape[2]
    slab, sub, rep = (lax.axis_index(axis) for axis in ("slab", "sub", "rep"))
    deep, tall = lax.axis_size("slab") * deep_count, lax.axis_size("sub") * tall_count
    rows = deep * tall
    replicas, receivers = replica_seeds.shape[0], receiver_z.shape[0]
    own_shape = (deep_count, tall_count, part_width)
    cube = (deep, tall, wide)
    last_rows = deep_count * tall_count + receivers
    block = min(rows, 256)
    smem = pl.BlockSpec(memory_space=pltpu.SMEM)
    vmem = pl.BlockSpec(memory_space=pltpu.VMEM)
    anywhere = pl.BlockSpec(memory_space=pltpu.HBM)

    def held(*shape, dtype=jnp.float32):
        return jax.ShapeDtypeStruct(shape, dtype)

    def call(kernel, out_shape, scalars, distant, arrays, scratch):
        return pl.pallas_call(
            kernel,
            out_shape=out_shape,
            in_specs=[smem] * len(scalars) + [anywhere] * len(distant) + [vmem] * len(arrays),
            out_specs=tuple(vmem for _ in out_shape),
            scratch_shapes=list(scratch),
            compiler_params=pltpu.CompilerParams(vmem_limit_bytes=24 * 2**20),
        )(*scalars, *(pltpu.with_memory_space_constraint(a, pltpu.HBM) for a in distant), *arrays)

    place = jnp.stack([slab, sub, rep]).astype(jnp.int32)
    given = (
        wavelet,
        source_z,
        source_y,
        source_x,
        replica_seeds,
        receiver_z,
        receiver_y,
        receiver_x,
    )
    prepared = call(
        functools.partial(prepare_kernel, own_shape[:2]),
        (
            held(replicas, *cube),
            held(STEPS - 1, *cube),
            held(replicas, last_rows, wide),
            held(last_rows, wide),
            held(rows // block, block + receivers, 3 * block, dtype=jnp.bfloat16),
            held(3 * wide, wide, dtype=jnp.bfloat16),
            held(last_rows + receivers, 3 * rows, dtype=jnp.bfloat16),
            held(receivers, wide),
        ),
        (place,),
        given,
        (),
        (
            *(pltpu.SMEM(array.shape, array.dtype) for array in given),
            pltpu.SemaphoreType.DMA((len(given),)),
        ),
    )
    own = call(
        pack_kernel,
        (held(4 * deep_count, tall_count, part_width),),
        (),
        (incident_now, incident_prev, courant),
        (),
        (pltpu.SemaphoreType.DMA((4,)),),
    )[0]
    blocks, layout, prepared = exchanged(own, deep_count, prepared)
    incident_final, scattered_final, traces = call(
        functools.partial(step_kernel, layout, own_shape),
        (
            held(*own_shape),
            held(replicas, deep_count, tall_count, wide),
            held(STEPS * replicas, receivers),
        ),
        (place,),
        (),
        (*prepared, *blocks),
        (
            pltpu.VMEM((4,) + cube, jnp.float32),
            pltpu.VMEM(cube, jnp.float32),
            pltpu.VMEM(cube, jnp.float32),
            pltpu.VMEM((replicas, 3) + cube, jnp.float32),
            pltpu.VMEM((2 + replicas, rows // block, 3 * block, wide), jnp.bfloat16),
            pltpu.VMEM((1 + replicas, rows // block, block, wide), jnp.float32),
            pltpu.VMEM((1 + replicas, rows // block, receivers, wide), jnp.float32),
            pltpu.VMEM((deep_count * tall_count, wide), jnp.float32),
        ),
    )
    return incident_final, scattered_final, traces.reshape(STEPS, replicas, receivers)


def solution(mesh):
    slabs, subs, reps = (mesh.shape[axis] for axis in ("slab", "sub", "rep"))

    def step(courant, *rest):
        deep, tall, _ = courant.shape
        paired = (slabs, subs, reps, mesh.shape["shot"]) == (4, 2, 2, 2)
        part_width = courant.shape[2] // reps
        fits = deep * tall <= GRID_ROWS and part_width % 128 == 0
        return jax.shard_map(
            whole_shards if paired and fits else halo_shards,
            mesh=mesh,
            in_specs=(
                P("slab", "sub", None),
                P(("shot", "slab"), "sub", "rep"),
                P(("shot", "slab"), "sub", "rep"),
                P(),
                P("shot"),
                P("shot"),
                P("shot"),
                P("rep"),
                P(),
                P(),
                P(),
            ),
            out_specs=(
                P(("shot", "slab"), "sub", "rep"),
                P("rep", ("shot", "slab"), "sub", None),
                P("shot", "rep", None),
            ),
            check_vma=False,
        )(courant, *rest)

    return step
```

```python
import functools

import jax
import jax.numpy as jnp
import numpy as np
from jax import lax
from jax.experimental import pallas as pl
from jax.experimental.pallas import tpu as pltpu
from jax.sharding import PartitionSpec as P

STEPS = 4
GRID_ROWS = 512
CHUNK = 2
WAVE_PARTS = 2


stencil_coeffs = (-205.0 / 72.0, 8.0 / 5.0, -1.0 / 5.0, 8.0 / 315.0, -1.0 / 560.0)
pert_scale = 0.2
whole_coeffs = (-14350, 8064, -1008, 128, -9)
coeff_scale = 5040.0


def padded_2(array, sides, width):
    for axis, dim in sides:
        size, length = (lax.axis_size(axis), array.shape[dim])
        up = [(i, (i + 1) % size) for i in range(size - 1)]
        down = [(j, i) for i, j in up]
        last = lax.slice_in_dim(array, length - width, length, axis=dim)
        first = lax.slice_in_dim(array, 0, width, axis=dim)
        before = lax.ppermute(last, axis, up)
        after = lax.ppermute(first, axis, down)
        array = jnp.concatenate([before, array, after], axis=dim)
    return array


def laplace(padded):
    deep_count = padded.shape[-3] - 8
    tall_count = padded.shape[-2] - 8
    wide_count = padded.shape[-1] - 8

    def window(shift_z, shift_y, shift_x):
        return padded[
            ...,
            4 + shift_z : 4 + shift_z + deep_count,
            4 + shift_y : 4 + shift_y + tall_count,
            4 + shift_x : 4 + shift_x + wide_count,
        ]

    summed = 3.0 * stencil_coeffs[0] * window(0, 0, 0)
    for offset in range(1, 5):
        couple = (
            window(offset, 0, 0)
            + window(-offset, 0, 0)
            + window(0, offset, 0)
            + window(0, -offset, 0)
            + window(0, 0, offset)
            + window(0, 0, -offset)
        )
        summed = summed + stencil_coeffs[offset] * couple
    return summed


def perturbation(seed_values, depth_coord, height_coord, width_coord):
    hashed = (
        seed_values[:, None, None, None] * 668265263
        + depth_coord[None, :, None, None] * 73856093
        + height_coord[None, None, :, None] * 19349663
        + width_coord[None, None, None, :] * 83492791
    )
    hashed = jnp.bitwise_xor(hashed, jnp.right_shift(hashed, 15))
    hashed = hashed * 1274126177
    hashed = jnp.bitwise_xor(hashed, jnp.right_shift(hashed, 13))
    fraction = jnp.bitwise_and(hashed, 65535).astype(jnp.float32) / 65535.0
    return pert_scale * (2.0 * fraction - 1.0)


def inject(field, amounts, where_z, where_y, where_x, start_z, start_y, start_x):
    local_z = where_z - start_z
    local_y = where_y - start_y
    local_x = where_x - start_x
    inside = (
        (local_z >= 0)
        & (local_z < field.shape[0])
        & (local_y >= 0)
        & (local_y < field.shape[1])
        & (local_x >= 0)
        & (local_x < field.shape[2])
    )
    clip_z = jnp.clip(local_z, 0, field.shape[0] - 1)
    clip_y = jnp.clip(local_y, 0, field.shape[1] - 1)
    clip_x = jnp.clip(local_x, 0, field.shape[2] - 1)
    return field.at[clip_z, clip_y, clip_x].add(jnp.where(inside, amounts, jnp.zeros_like(amounts)))


def sample(field, where_z, where_y, where_x, start_z, start_y):
    local_z = where_z - start_z
    local_y = where_y - start_y
    inside = (
        (local_z >= 0) & (local_z < field.shape[1]) & (local_y >= 0) & (local_y < field.shape[2])
    )
    clip_z = jnp.clip(local_z, 0, field.shape[1] - 1)
    clip_y = jnp.clip(local_y, 0, field.shape[2] - 1)
    picked = field[:, clip_z, clip_y, where_x]
    return jnp.where(inside[None, :], picked, jnp.zeros_like(picked))


def halo_shards(
    courant,
    incident_prev,
    incident_now,
    wavelet,
    source_z,
    source_y,
    source_x,
    replica_seeds,
    receiver_z,
    receiver_y,
    receiver_x,
):
    deep_count, tall_count, part_width = incident_now.shape
    full_width = courant.shape[2]
    start_z = lax.axis_index("slab") * deep_count
    start_y = lax.axis_index("sub") * tall_count
    start_x = lax.axis_index("rep") * part_width
    speed_square = courant * courant
    depth_coord = start_z + jnp.arange(deep_count, dtype=jnp.int32)
    height_coord = start_y + jnp.arange(tall_count, dtype=jnp.int32)
    width_coord = jnp.arange(full_width, dtype=jnp.int32)
    contrast = perturbation(replica_seeds, depth_coord, height_coord, width_coord)
    whole_prev, whole_now = (
        lax.all_gather(incident_prev, "rep", axis=2, tiled=True),
        lax.all_gather(incident_now, "rep", axis=2, tiled=True),
    )
    wave_prev = jnp.zeros(contrast.shape, jnp.float32)
    wave_now = jnp.zeros(contrast.shape, jnp.float32)
    recorded = []
    for step_index in range(STEPS):
        padded = padded_2(whole_now, (("slab", 0), ("sub", 1)), 4)
        padded = jnp.pad(padded, ((0, 0), (0, 0), (4, 4)))
        whole_next = 2.0 * whole_now - whole_prev + speed_square * laplace(padded)
        whole_next = inject(
            whole_next, wavelet[step_index], source_z, source_y, source_x, start_z, start_y, 0
        )
        wave_padded = padded_2(wave_now, (("slab", 1), ("sub", 2)), 4)
        wave_padded = jnp.pad(wave_padded, ((0, 0), (0, 0), (0, 0), (4, 4)))
        source_term = 2.0 * contrast * (whole_next - 2.0 * whole_now + whole_prev)
        whole_prev, whole_now = (whole_now, whole_next)
        wave_next = 2.0 * wave_now - wave_prev + speed_square * laplace(wave_padded) + source_term
        picked = sample(wave_next, receiver_z, receiver_y, receiver_x, start_z, start_y)
        picked = lax.psum(picked, ("slab", "sub"))
        recorded.append(picked)
        wave_prev, wave_now = (wave_now, wave_next)
    traces = jnp.stack(recorded)
    incident_final = lax.dynamic_slice_in_dim(whole_now, start_x, part_width, 2)
    return (incident_final, wave_now, traces)


def band(apart):
    value = jnp.zeros(apart.shape, jnp.float32)
    for k in range(1, 5):
        value = jnp.where(apart == k, float(whole_coeffs[k]), value)
    return value


def split(value, count):
    parts = []
    for part in range(count):
        parts.append(value.astype(jnp.bfloat16))
        if part < count - 1:
            value = value - parts[-1].astype(jnp.float32)
    return parts


def product(left, right):
    return jnp.dot(left, right, preferred_element_type=jnp.float32)


def across(row, column, tall):
    far_z = jnp.abs(lax.div(row, tall) - lax.div(column, tall))
    far_y = jnp.abs(lax.rem(row, tall) - lax.rem(column, tall))
    return band(jnp.where(far_y == 0, far_z, jnp.where(far_z == 0, far_y, 0)))


def doubled_contrast(cell, seed):
    hashed = cell + seed * 668265263
    hashed = hashed ^ (hashed >> 15)
    hashed = hashed * 1274126177
    hashed = hashed ^ (hashed >> 13)
    fraction = (hashed & 65535).astype(jnp.float32) / 65535.0
    return 2.0 * (pert_scale * (2.0 * fraction - 1.0))


def fetched(sources, targets, semaphores):
    copies = [
        pltpu.make_async_copy(source, target, semaphores.at[i])
        for i, (source, target) in enumerate(zip(sources, targets, strict=True))
    ]
    for copy in copies:
        copy.start()
    return copies


def pack_kernel(now_ref, prev_ref, courant_ref, own_ref, semaphores):
    layers, _, part_width = now_ref.shape
    rep = lax.axis_index("rep")
    sources = [now_ref, prev_ref]
    for x in range(2):
        at_x = pl.multiple_of((rep ^ x) * part_width, part_width)
        sources.append(courant_ref.at[:, :, pl.ds(at_x, part_width)])
    targets = [own_ref.at[pl.ds(i * layers, layers)] for i in range(4)]
    for copy in fetched(sources, targets, semaphores):
        copy.wait()


def beside_kernel(wide_ref):
    wide = wide_ref.shape[1]
    line = lax.broadcasted_iota(jnp.int32, (wide, wide), 0)
    beside = band(jnp.abs(line - lax.broadcasted_iota(jnp.int32, (wide, wide), 1)))
    for part in range(3):
        wide_ref[part * wide : (part + 1) * wide, :] = beside.astype(jnp.bfloat16)


def prepare_kernel(own_shape, *refs):
    place_ref, refs = refs[0], refs[1:]
    given, outputs, held, semaphores = refs[:8], refs[8:15], refs[15:23], refs[23]
    contrast_ref, force_ref, last_contrast_ref, last_force_ref = outputs[:4]
    rows_ref, last_ref, mask_ref = outputs[4:]
    wavelet_ref, source_z_ref, source_y_ref, source_x_ref = held[:4]
    seeds_ref, receiver_z_ref, receiver_y_ref, receiver_x_ref = held[4:]
    copies = fetched(given, held, semaphores)
    deep, tall, wide = force_ref.shape[1:]
    rows = deep * tall
    runs, tops, block = rows_ref.shape[0], rows_ref.shape[1], rows_ref.shape[2] // 3
    receivers = mask_ref.shape[0]
    deep_count, tall_count = own_shape
    own = deep_count * tall_count
    replicas = seeds_ref.shape[0]
    sources = range(source_z_ref.shape[0])
    for copy in copies:
        copy.wait()
    z_of = lax.broadcasted_iota(jnp.int32, (deep, tall, wide), 0)
    y_of = lax.broadcasted_iota(jnp.int32, (deep, tall, wide), 1)
    x_of = lax.broadcasted_iota(jnp.int32, (deep, tall, wide), 2)
    cell = z_of * 73856093 + y_of * 19349663 + x_of * 83492791
    for r in range(replicas):
        contrast_ref[r] = doubled_contrast(cell, seeds_ref[r])
    lane = lax.broadcasted_iota(jnp.int32, (1, wide), 1)
    force_ref[...] = jnp.zeros_like(force_ref)
    for n in range(STEPS - 1):
        for k in sources:
            at = (n, source_z_ref[k], pl.ds(source_y_ref[k], 1), slice(None))
            force_ref[at] += jnp.where(lane == source_x_ref[k], wavelet_ref[n, k], 0.0)
    index = lax.broadcasted_iota(jnp.int32, (own + receivers, 1), 0)
    row = (place_ref[0] * deep_count + lax.div(index, tall_count)) * tall
    row += place_ref[1] * tall_count + lax.rem(index, tall_count)
    for j in range(receivers):
        row = jnp.where(index == own + j, receiver_z_ref[j] * tall + receiver_y_ref[j], row)
        mask_ref[pl.ds(j, 1), :] = jnp.where(lane == receiver_x_ref[j], 1.0, 0.0)
    cell = lax.div(row, tall) * 73856093 + lax.rem(row, tall) * 19349663 + lane * 83492791
    for r in range(replicas):
        last_contrast_ref[r] = doubled_contrast(cell, seeds_ref[r])
    force = jnp.zeros((own + receivers, wide), jnp.float32)
    for k in sources:
        here = (row == source_z_ref[k] * tall + source_y_ref[k]) & (lane == source_x_ref[k])
        force += jnp.where(here, wavelet_ref[STEPS - 1, k], 0.0)
    last_force_ref[...] = force
    column = lax.broadcasted_iota(jnp.int32, (1, rows), 1)
    taken = jnp.where(row[own:] == column, 1.0, 0.0)
    last = jnp.concatenate([across(row, column, tall), taken], axis=0).astype(jnp.bfloat16)
    line = lax.broadcasted_iota(jnp.int32, (block, 1), 0)
    inner = across(line, column[:, :block], tall).astype(jnp.bfloat16)
    for part in range(3):
        for run in range(runs):
            start = (3 * run + part) * block
            last_ref[:, start : start + block] = last[:, run * block : (run + 1) * block]
            here = (run, slice(0, block), slice(part * block, (part + 1) * block))
            rows_ref[here] = inner
            here = (run, slice(block, tops), slice(part * block, (part + 1) * block))
            rows_ref[here] = taken[:, run * block : (run + 1) * block].astype(jnp.bfloat16)


def step_kernel(
    layout,
    own_shape,
    place_ref,
    contrast_ref,
    force_ref,
    last_contrast_ref,
    last_force_ref,
    rows_ref,
    last_ref,
    mask_ref,
    wide_ref,
    *refs,
):
    blocks, refs = refs[:-11], refs[-11:]
    incident_ref, scattered_ref, traces_ref = refs[:3]
    field_ref, speed_ref, drive_ref, wave_ref, parts_ref, product_ref, taken_ref, slim_ref = refs[3:]
    deep, tall, wide = speed_ref.shape
    deep_count, tall_count, part_width = own_shape
    own = deep_count * tall_count
    replicas = contrast_ref.shape[0]
    receivers = mask_ref.shape[0]
    runs, block = rows_ref.shape[0], rows_ref.shape[2] // 3
    run = block // tall
    group = min(run, CHUNK)
    slab, sub, rep = (place_ref[i] for i in range(3))

    for number, layer, what, x, y, z in layout:
        half = rep ^ x
        at = (
            pl.ds(pl.multiple_of((slab ^ z) * deep_count, deep_count), deep_count),
            pl.ds(pl.multiple_of((sub ^ y) * tall_count, tall_count), tall_count),
            pl.ds(pl.multiple_of(half * part_width, part_width), part_width),
        )
        piece = blocks[number][layer : layer + deep_count]
        if what == "courant":
            speed_ref[at] = piece * piece * (1.0 / coeff_scale)
        else:
            field_ref[(("prev", "now").index(what),) + at] = piece

    def groups(number):
        for first in range(number * run, (number + 1) * run, group):
            yield first, slice((first - number * run) * tall, (first - number * run + group) * tall)

    def flat(ref, *index):
        value = ref[index]
        return value.reshape(-1, wide)

    def near(ref, first, *index):
        return flat(ref, *index, slice(first, first + group))

    def put(ref, value, first, *index):
        ref[index + (slice(first, first + group),)] = value.reshape(group, tall, wide)

    def cut(slot, number, rows, value, count):
        for part, piece in enumerate(split(value, count)):
            parts_ref[slot, number, part * block + rows.start : part * block + rows.stop] = piece

    def multiply(slot, number, count, sampled):
        held = parts_ref[slot, number, : count * block]
        tops = rows_ref.shape[1] if sampled else block
        beside = jnp.concatenate([held[part * block : (part + 1) * block] for part in range(count)], axis=1)
        down = product(rows_ref[number, :tops, : count * block], held)
        product_ref[slot, number] = down[:block] + product(beside, wide_ref[: count * wide])
        if sampled:
            taken_ref[slot, number] = down[block:]

    def applied(slot, number, rows, first, ref, *index):
        total = (3.0 * whole_coeffs[0]) * near(ref, first, *index) + product_ref[slot, number, rows]
        pieces = []
        for z in range(first, first + group):
            piece = total[(z - first) * tall : (z - first + 1) * tall]
            for k in range(1, 5):
                for other in (z - k, z + k):
                    if 0 <= other < deep and other // run != z // run:
                        piece = piece + float(whole_coeffs[k]) * ref[index + (other,)]
            pieces.append(piece)
        return jnp.concatenate(pieces, axis=0) if len(pieces) > 1 else pieces[0]

    def start_incident(number):
        for first, rows in groups(number):
            cut(0, number, rows, near(field_ref, first, 1), 3)

    def step_incident(n, number):
        before, now, after = n % 4, (n + 1) % 4, (n + 2) % 4
        for first, rows in groups(number):
            drive = near(speed_ref, first) * applied(0, number, rows, first, field_ref, now)
            drive += near(force_ref, first, n)
            put(drive_ref, drive, first)
            following = 2.0 * near(field_ref, first, now) - near(field_ref, first, before) + drive
            put(field_ref, following, first, after)
            cut(0, number, rows, following, 3)
            if n == 0:
                for r in range(replicas):
                    wave = near(contrast_ref, first, r) * drive
                    put(wave_ref, wave, first, r, 0)
                    cut(1 + r, number, rows, wave, WAVE_PARTS)

    def step_wave(n, r, number):
        for first, rows in groups(number):
            following = (
                2.0 * near(wave_ref, first, r, n - 1)
                + near(speed_ref, first) * applied(1 + r, number, rows, first, wave_ref, r, n - 1)
                + near(contrast_ref, first, r) * near(drive_ref, first)
            )
            if n > 1:
                following -= near(wave_ref, first, r, n - 2)
            put(wave_ref, following, first, r, n)
            cut(1 + r, number, rows, following, WAVE_PARTS)

    at_z = pl.multiple_of(slab * deep_count, deep_count)
    at_y = pl.multiple_of(sub * tall_count, tall_count)
    at_x = pl.multiple_of(rep * part_width, part_width)

    def owned(ref, *index):
        here = index + (pl.ds(at_z, deep_count), pl.ds(at_y, tall_count), slice(None))
        return ref[here].reshape(own, wide)

    def chosen(slot, rows, count):
        total = None
        for number in range(runs):
            start = number * 3 * block
            held = parts_ref[slot, number, : count * block]
            term = product(last_ref[rows, start : start + count * block], held)
            total = term if total is None else total + term
        return total

    samples = [[None] * replicas for _ in range(STEPS)]
    each = range(runs)

    for number in each:
        start_incident(number)
    for number in each:
        multiply(0, number, 3, False)
    for number in each:
        for first, rows in groups(number):
            cut(1 + replicas, number, rows, near(speed_ref, first), 3)
    for number in each:
        step_incident(0, number)
    for n in (1, 2):
        work = [(multiply, (0, number, 3, False)) for number in each]
        after = [(step_incident, (n, number)) for number in each]
        for r in range(replicas):
            work += [(multiply, (1 + r, number, WAVE_PARTS, True)) for number in each]
            after += [(step_wave, (n, r, number)) for number in each]
        for i in range(len(work) + runs):
            if i < len(work):
                work[i][0](*work[i][1])
            if i >= runs:
                after[i - runs][0](*after[i - runs][1])
        for r in range(replicas):
            samples[n - 1][r] = sum(taken_ref[1 + r, number] for number in each)

    receiver_rows = slice(own + receivers, own + 2 * receivers)
    speed = jnp.concatenate([owned(speed_ref), chosen(1 + replicas, receiver_rows, 3)], axis=0)

    def last_applied(slot, mine, count):
        result = chosen(slot, slice(None), count)
        here = jnp.concatenate([mine, result[own + receivers :]], axis=0)
        total = (3.0 * whole_coeffs[0]) * here + result[: own + receivers]
        beside = jnp.concatenate(split(here, count), axis=1)
        return total + product(beside, wide_ref[: count * wide]), here

    result, now = last_applied(0, owned(field_ref, 0), 3)
    drive = speed * result + last_force_ref[...]
    slim_ref[...] = 2.0 * now[:own] - owned(field_ref, 3) + drive[:own]
    incident_ref[...] = slim_ref[:, pl.ds(at_x, part_width)].reshape(incident_ref.shape)
    for r in range(replicas):
        result, wave = last_applied(1 + r, owned(wave_ref, r, 2), WAVE_PARTS)
        samples[2][r] = wave[own:]
        before = jnp.concatenate([owned(wave_ref, r, 1), samples[1][r]], axis=0)
        following = 2.0 * wave - before + speed * result + last_contrast_ref[r] * drive
        scattered_ref[r] = following[:own].reshape(scattered_ref.shape[1:])
        samples[3][r] = following[own:]
    column = lax.broadcasted_iota(jnp.int32, (receivers, 128), 1)
    gathered = jnp.zeros((receivers, 128), jnp.float32)
    mask = mask_ref[...]
    for n in range(STEPS):
        for r in range(replicas):
            summed = jnp.sum(samples[n][r] * mask, axis=1, keepdims=True)
            gathered += jnp.where(column == n * replicas + r, summed, 0.0)
    traces_ref[...] = jnp.transpose(gathered)[: STEPS * replicas, :]


def swapped(array, axis, distance):
    size = lax.axis_size(axis)
    return lax.ppermute(array, axis, [(i, i ^ distance) for i in range(size)])


def exchanged(own, deep_count, matrices, prepared):
    sent = own[: 3 * deep_count]
    beyond = {m: swapped(sent, "slab", m) for m in (1, 2)}
    late, matrices = lax.optimization_barrier((sent, matrices))
    beyond[3] = swapped(late, "slab", 3)
    near = jnp.concatenate([own[: 2 * deep_count], beyond[1]], axis=0)
    near_two, two_two = swapped(near, "rep", 1), swapped(beyond[2], "rep", 1)
    near_two, prepared = lax.optimization_barrier((near_two, prepared))
    three_two = swapped(beyond[3], "rep", 1)
    blocks = [
        jnp.concatenate([near, near_two, own[2 * deep_count :]], axis=0),
        jnp.concatenate([beyond[2], two_two], axis=0),
        jnp.concatenate([beyond[3], three_two], axis=0),
    ]
    blocks += [swapped(block, "sub", 1) for block in blocks]
    names = ("now", "prev", "courant")
    near_layout = [(name, 0) for name in names[:2]] + [(name, 1) for name in names]
    layouts = [[(name, x, z) for x in range(2) for name, z in near_layout]]
    layouts[0] += [("courant", x, 0) for x in range(2)]
    layouts += [[(name, x, z) for x in range(2) for name in names] for z in (2, 3)]
    layout = [
        (len(layouts) * y + number, i * deep_count, name, x, y, z)
        for y in range(2)
        for number, parts in enumerate(layouts)
        for i, (name, x, z) in enumerate(parts)
    ]
    return blocks, tuple(layout), (*prepared, *matrices)


def whole_shards(
    courant,
    incident_prev,
    incident_now,
    wavelet,
    source_z,
    source_y,
    source_x,
    replica_seeds,
    receiver_z,
    receiver_y,
    receiver_x,
):
    deep_count, tall_count, part_width = incident_now.shape
    wide = courant.shape[2]
    slab, sub, rep = (lax.axis_index(axis) for axis in ("slab", "sub", "rep"))
    deep, tall = lax.axis_size("slab") * deep_count, lax.axis_size("sub") * tall_count
    rows = deep * tall
    replicas, receivers = replica_seeds.shape[0], receiver_z.shape[0]
    own_shape = (deep_count, tall_count, part_width)
    cube = (deep, tall, wide)
    last_rows = deep_count * tall_count + receivers
    block = min(rows, 256)
    smem = pl.BlockSpec(memory_space=pltpu.SMEM)
    vmem = pl.BlockSpec(memory_space=pltpu.VMEM)
    anywhere = pl.BlockSpec(memory_space=pltpu.HBM)

    def held(*shape, dtype=jnp.float32):
        return jax.ShapeDtypeStruct(shape, dtype)

    def call(kernel, out_shape, scalars, distant, arrays, scratch):
        return pl.pallas_call(
            kernel,
            out_shape=out_shape,
            in_specs=[smem] * len(scalars) + [anywhere] * len(distant) + [vmem] * len(arrays),
            out_specs=tuple(vmem for _ in out_shape),
            scratch_shapes=list(scratch),
            compiler_params=pltpu.CompilerParams(vmem_limit_bytes=24 * 2**20),
        )(*scalars, *(pltpu.with_memory_space_constraint(a, pltpu.HBM) for a in distant), *arrays)

    place = jnp.stack([slab, sub, rep]).astype(jnp.int32)
    given = (
        wavelet,
        source_z,
        source_y,
        source_x,
        replica_seeds,
        receiver_z,
        receiver_y,
        receiver_x,
    )
    prepared = call(
        functools.partial(prepare_kernel, own_shape[:2]),
        (
            held(replicas, *cube),
            held(STEPS - 1, *cube),
            held(replicas, last_rows, wide),
            held(last_rows, wide),
            held(rows // block, block + receivers, 3 * block, dtype=jnp.bfloat16),
            held(last_rows + receivers, 3 * rows, dtype=jnp.bfloat16),
            held(receivers, wide),
        ),
        (place,),
        given,
        (),
        (
            *(pltpu.SMEM(array.shape, array.dtype) for array in given),
            pltpu.SemaphoreType.DMA((len(given),)),
        ),
    )
    matrices = call(beside_kernel, (held(3 * wide, wide, dtype=jnp.bfloat16),), (), (), (), ())
    own = call(
        pack_kernel,
        (held(4 * deep_count, tall_count, part_width),),
        (),
        (incident_now, incident_prev, courant),
        (),
        (pltpu.SemaphoreType.DMA((4,)),),
    )[0]
    blocks, layout, prepared = exchanged(own, deep_count, matrices, prepared)
    incident_final, scattered_final, traces = call(
        functools.partial(step_kernel, layout, own_shape),
        (
            held(*own_shape),
            held(replicas, deep_count, tall_count, wide),
            held(STEPS * replicas, receivers),
        ),
        (place,),
        (),
        (*prepared, *blocks),
        (
            pltpu.VMEM((4,) + cube, jnp.float32),
            pltpu.VMEM(cube, jnp.float32),
            pltpu.VMEM(cube, jnp.float32),
            pltpu.VMEM((replicas, 3) + cube, jnp.float32),
            pltpu.VMEM((2 + replicas, rows // block, 3 * block, wide), jnp.bfloat16),
            pltpu.VMEM((1 + replicas, rows // block, block, wide), jnp.float32),
            pltpu.VMEM((1 + replicas, rows // block, receivers, wide), jnp.float32),
            pltpu.VMEM((deep_count * tall_count, wide), jnp.float32),
        ),
    )
    return incident_final, scattered_final, traces.reshape(STEPS, replicas, receivers)


def solution(mesh):
    slabs, subs, reps = (mesh.shape[axis] for axis in ("slab", "sub", "rep"))

    def step(courant, *rest):
        deep, tall, _ = courant.shape
        paired = (slabs, subs, reps, mesh.shape["shot"]) == (4, 2, 2, 2)
        part_width = courant.shape[2] // reps
        fits = deep * tall <= GRID_ROWS and part_width % 128 == 0
        return jax.shard_map(
            whole_shards if paired and fits else halo_shards,
            mesh=mesh,
            in_specs=(
                P("slab", "sub", None),
                P(("shot", "slab"), "sub", "rep"),
                P(("shot", "slab"), "sub", "rep"),
                P(),
                P("shot"),
                P("shot"),
                P("shot"),
                P("rep"),
                P(),
                P(),
                P(),
            ),
            out_specs=(
                P(("shot", "slab"), "sub", "rep"),
                P("rep", ("shot", "slab"), "sub", None),
                P("shot", "rep", None),
            ),
            check_vma=False,
        )(courant, *rest)

    return step
```

```python
import functools

import jax
import jax.numpy as jnp
import numpy as np
from jax import lax
from jax.experimental import pallas as pl
from jax.experimental.pallas import tpu as pltpu
from jax.sharding import PartitionSpec as P

STEPS = 4
GRID_ROWS = 512
CHUNK = 2
WAVE_PARTS = 2


stencil_coeffs = (-205.0 / 72.0, 8.0 / 5.0, -1.0 / 5.0, 8.0 / 315.0, -1.0 / 560.0)
pert_scale = 0.2
whole_coeffs = (-14350, 8064, -1008, 128, -9)
coeff_scale = 5040.0


def padded_2(array, sides, width):
    for axis, dim in sides:
        size, length = (lax.axis_size(axis), array.shape[dim])
        up = [(i, (i + 1) % size) for i in range(size - 1)]
        down = [(j, i) for i, j in up]
        last = lax.slice_in_dim(array, length - width, length, axis=dim)
        first = lax.slice_in_dim(array, 0, width, axis=dim)
        before = lax.ppermute(last, axis, up)
        after = lax.ppermute(first, axis, down)
        array = jnp.concatenate([before, array, after], axis=dim)
    return array


def laplace(padded):
    deep_count = padded.shape[-3] - 8
    tall_count = padded.shape[-2] - 8
    wide_count = padded.shape[-1] - 8

    def window(shift_z, shift_y, shift_x):
        return padded[
            ...,
            4 + shift_z : 4 + shift_z + deep_count,
            4 + shift_y : 4 + shift_y + tall_count,
            4 + shift_x : 4 + shift_x + wide_count,
        ]

    summed = 3.0 * stencil_coeffs[0] * window(0, 0, 0)
    for offset in range(1, 5):
        couple = (
            window(offset, 0, 0)
            + window(-offset, 0, 0)
            + window(0, offset, 0)
            + window(0, -offset, 0)
            + window(0, 0, offset)
            + window(0, 0, -offset)
        )
        summed = summed + stencil_coeffs[offset] * couple
    return summed


def perturbation(seed_values, depth_coord, height_coord, width_coord):
    hashed = (
        seed_values[:, None, None, None] * 668265263
        + depth_coord[None, :, None, None] * 73856093
        + height_coord[None, None, :, None] * 19349663
        + width_coord[None, None, None, :] * 83492791
    )
    hashed = jnp.bitwise_xor(hashed, jnp.right_shift(hashed, 15))
    hashed = hashed * 1274126177
    hashed = jnp.bitwise_xor(hashed, jnp.right_shift(hashed, 13))
    fraction = jnp.bitwise_and(hashed, 65535).astype(jnp.float32) / 65535.0
    return pert_scale * (2.0 * fraction - 1.0)


def inject(field, amounts, where_z, where_y, where_x, start_z, start_y, start_x):
    local_z = where_z - start_z
    local_y = where_y - start_y
    local_x = where_x - start_x
    inside = (
        (local_z >= 0)
        & (local_z < field.shape[0])
        & (local_y >= 0)
        & (local_y < field.shape[1])
        & (local_x >= 0)
        & (local_x < field.shape[2])
    )
    clip_z = jnp.clip(local_z, 0, field.shape[0] - 1)
    clip_y = jnp.clip(local_y, 0, field.shape[1] - 1)
    clip_x = jnp.clip(local_x, 0, field.shape[2] - 1)
    return field.at[clip_z, clip_y, clip_x].add(jnp.where(inside, amounts, jnp.zeros_like(amounts)))


def sample(field, where_z, where_y, where_x, start_z, start_y):
    local_z = where_z - start_z
    local_y = where_y - start_y
    inside = (
        (local_z >= 0) & (local_z < field.shape[1]) & (local_y >= 0) & (local_y < field.shape[2])
    )
    clip_z = jnp.clip(local_z, 0, field.shape[1] - 1)
    clip_y = jnp.clip(local_y, 0, field.shape[2] - 1)
    picked = field[:, clip_z, clip_y, where_x]
    return jnp.where(inside[None, :], picked, jnp.zeros_like(picked))


def halo_shards(
    courant,
    incident_prev,
    incident_now,
    wavelet,
    source_z,
    source_y,
    source_x,
    replica_seeds,
    receiver_z,
    receiver_y,
    receiver_x,
):
    deep_count, tall_count, part_width = incident_now.shape
    full_width = courant.shape[2]
    start_z = lax.axis_index("slab") * deep_count
    start_y = lax.axis_index("sub") * tall_count
    start_x = lax.axis_index("rep") * part_width
    speed_square = courant * courant
    depth_coord = start_z + jnp.arange(deep_count, dtype=jnp.int32)
    height_coord = start_y + jnp.arange(tall_count, dtype=jnp.int32)
    width_coord = jnp.arange(full_width, dtype=jnp.int32)
    contrast = perturbation(replica_seeds, depth_coord, height_coord, width_coord)
    whole_prev, whole_now = (
        lax.all_gather(incident_prev, "rep", axis=2, tiled=True),
        lax.all_gather(incident_now, "rep", axis=2, tiled=True),
    )
    wave_prev = jnp.zeros(contrast.shape, jnp.float32)
    wave_now = jnp.zeros(contrast.shape, jnp.float32)
    recorded = []
    for step_index in range(STEPS):
        padded = padded_2(whole_now, (("slab", 0), ("sub", 1)), 4)
        padded = jnp.pad(padded, ((0, 0), (0, 0), (4, 4)))
        whole_next = 2.0 * whole_now - whole_prev + speed_square * laplace(padded)
        whole_next = inject(
            whole_next, wavelet[step_index], source_z, source_y, source_x, start_z, start_y, 0
        )
        wave_padded = padded_2(wave_now, (("slab", 1), ("sub", 2)), 4)
        wave_padded = jnp.pad(wave_padded, ((0, 0), (0, 0), (0, 0), (4, 4)))
        source_term = 2.0 * contrast * (whole_next - 2.0 * whole_now + whole_prev)
        whole_prev, whole_now = (whole_now, whole_next)
        wave_next = 2.0 * wave_now - wave_prev + speed_square * laplace(wave_padded) + source_term
        picked = sample(wave_next, receiver_z, receiver_y, receiver_x, start_z, start_y)
        picked = lax.psum(picked, ("slab", "sub"))
        recorded.append(picked)
        wave_prev, wave_now = (wave_now, wave_next)
    traces = jnp.stack(recorded)
    incident_final = lax.dynamic_slice_in_dim(whole_now, start_x, part_width, 2)
    return (incident_final, wave_now, traces)


def band(apart):
    value = jnp.zeros(apart.shape, jnp.float32)
    for k in range(1, 5):
        value = jnp.where(apart == k, float(whole_coeffs[k]), value)
    return value


def split(value, count):
    parts = []
    for part in range(count):
        parts.append(value.astype(jnp.bfloat16))
        if part < count - 1:
            value = value - parts[-1].astype(jnp.float32)
    return parts


def product(left, right):
    return jnp.dot(left, right, preferred_element_type=jnp.float32)


def across(row, column, tall):
    far_z = jnp.abs(lax.div(row, tall) - lax.div(column, tall))
    far_y = jnp.abs(lax.rem(row, tall) - lax.rem(column, tall))
    return band(jnp.where(far_y == 0, far_z, jnp.where(far_z == 0, far_y, 0)))


def doubled_contrast(cell, seed):
    hashed = cell + seed * 668265263
    hashed = hashed ^ (hashed >> 15)
    hashed = hashed * 1274126177
    hashed = hashed ^ (hashed >> 13)
    fraction = (hashed & 65535).astype(jnp.float32) / 65535.0
    return 2.0 * (pert_scale * (2.0 * fraction - 1.0))


def fetched(sources, targets, semaphores):
    copies = [
        pltpu.make_async_copy(source, target, semaphores.at[i])
        for i, (source, target) in enumerate(zip(sources, targets, strict=True))
    ]
    for copy in copies:
        copy.start()
    return copies


def pack_kernel(now_ref, prev_ref, courant_ref, own_ref, semaphores):
    layers, _, part_width = now_ref.shape
    rep = lax.axis_index("rep")
    sources = [now_ref, prev_ref]
    for x in range(2):
        at_x = pl.multiple_of((rep ^ x) * part_width, part_width)
        sources.append(courant_ref.at[:, :, pl.ds(at_x, part_width)])
    targets = [own_ref.at[pl.ds(i * layers, layers)] for i in range(4)]
    for copy in fetched(sources, targets, semaphores):
        copy.wait()


def beside_kernel(wide_ref):
    wide = wide_ref.shape[1]
    line = lax.broadcasted_iota(jnp.int32, (wide, wide), 0)
    beside = band(jnp.abs(line - lax.broadcasted_iota(jnp.int32, (wide, wide), 1)))
    for part in range(3):
        wide_ref[part * wide : (part + 1) * wide, :] = beside.astype(jnp.bfloat16)


def prepare_kernel(own_shape, *refs):
    given, outputs, held, semaphores = refs[:8], refs[8:15], refs[15:23], refs[23]
    contrast_ref, force_ref, last_contrast_ref, last_force_ref = outputs[:4]
    rows_ref, last_ref, mask_ref = outputs[4:]
    wavelet_ref, source_z_ref, source_y_ref, source_x_ref = held[:4]
    seeds_ref, receiver_z_ref, receiver_y_ref, receiver_x_ref = held[4:]
    copies = fetched(given, held, semaphores)
    deep, tall, wide = force_ref.shape[1:]
    rows = deep * tall
    runs, tops, block = rows_ref.shape[0], rows_ref.shape[1], rows_ref.shape[2] // 3
    receivers = mask_ref.shape[0]
    deep_count, tall_count = own_shape
    own = deep_count * tall_count
    replicas = seeds_ref.shape[0]
    sources = range(source_z_ref.shape[0])
    for copy in copies:
        copy.wait()
    z_of = lax.broadcasted_iota(jnp.int32, (deep, tall, wide), 0)
    y_of = lax.broadcasted_iota(jnp.int32, (deep, tall, wide), 1)
    x_of = lax.broadcasted_iota(jnp.int32, (deep, tall, wide), 2)
    cell = z_of * 73856093 + y_of * 19349663 + x_of * 83492791
    for r in range(replicas):
        contrast_ref[r] = doubled_contrast(cell, seeds_ref[r])
    lane = lax.broadcasted_iota(jnp.int32, (1, wide), 1)
    force_ref[...] = jnp.zeros_like(force_ref)
    for n in range(STEPS - 1):
        for k in sources:
            at = (n, source_z_ref[k], pl.ds(source_y_ref[k], 1), slice(None))
            force_ref[at] += jnp.where(lane == source_x_ref[k], wavelet_ref[n, k], 0.0)
    index = lax.broadcasted_iota(jnp.int32, (own + receivers, 1), 0)
    row = (lax.axis_index("slab") * deep_count + lax.div(index, tall_count)) * tall
    row += lax.axis_index("sub") * tall_count + lax.rem(index, tall_count)
    for j in range(receivers):
        row = jnp.where(index == own + j, receiver_z_ref[j] * tall + receiver_y_ref[j], row)
        mask_ref[pl.ds(j, 1), :] = jnp.where(lane == receiver_x_ref[j], 1.0, 0.0)
    cell = lax.div(row, tall) * 73856093 + lax.rem(row, tall) * 19349663 + lane * 83492791
    for r in range(replicas):
        last_contrast_ref[r] = doubled_contrast(cell, seeds_ref[r])
    force = jnp.zeros((own + receivers, wide), jnp.float32)
    for k in sources:
        here = (row == source_z_ref[k] * tall + source_y_ref[k]) & (lane == source_x_ref[k])
        force += jnp.where(here, wavelet_ref[STEPS - 1, k], 0.0)
    last_force_ref[...] = force
    column = lax.broadcasted_iota(jnp.int32, (1, rows), 1)
    taken = jnp.where(row[own:] == column, 1.0, 0.0)
    last = jnp.concatenate([across(row, column, tall), taken], axis=0).astype(jnp.bfloat16)
    line = lax.broadcasted_iota(jnp.int32, (block, 1), 0)
    inner = across(line, column[:, :block], tall).astype(jnp.bfloat16)
    for part in range(3):
        for run in range(runs):
            start = (3 * run + part) * block
            last_ref[:, start : start + block] = last[:, run * block : (run + 1) * block]
            here = (run, slice(0, block), slice(part * block, (part + 1) * block))
            rows_ref[here] = inner
            here = (run, slice(block, tops), slice(part * block, (part + 1) * block))
            rows_ref[here] = taken[:, run * block : (run + 1) * block].astype(jnp.bfloat16)


def step_kernel(
    layout,
    own_shape,
    contrast_ref,
    force_ref,
    last_contrast_ref,
    last_force_ref,
    rows_ref,
    last_ref,
    mask_ref,
    wide_ref,
    *refs,
):
    blocks, refs = refs[:-15], refs[-15:]
    outputs = refs[:3]
    field_ref, speed_ref, drive_ref, wave_ref, parts_ref, product_ref, taken_ref, slim_ref = refs[3:11]
    incident_ref, scattered_ref, traces_ref, semaphores = refs[11:]
    copies = []

    def send(source, target):
        copies.append(pltpu.make_async_copy(source, target, semaphores.at[len(copies)]))
        copies[-1].start()

    deep, tall, wide = speed_ref.shape
    deep_count, tall_count, part_width = own_shape
    own = deep_count * tall_count
    replicas = contrast_ref.shape[0]
    receivers = mask_ref.shape[0]
    runs, block = rows_ref.shape[0], rows_ref.shape[2] // 3
    run = block // tall
    group = min(run, CHUNK)
    slab, sub, rep = (lax.axis_index(axis) for axis in ("slab", "sub", "rep"))

    for number, layer, what, x, y, z in layout:
        half = rep ^ x
        at = (
            pl.ds(pl.multiple_of((slab ^ z) * deep_count, deep_count), deep_count),
            pl.ds(pl.multiple_of((sub ^ y) * tall_count, tall_count), tall_count),
            pl.ds(pl.multiple_of(half * part_width, part_width), part_width),
        )
        piece = blocks[number][layer : layer + deep_count]
        if what == "courant":
            speed_ref[at] = piece * piece * (1.0 / coeff_scale)
        else:
            field_ref[(("prev", "now").index(what),) + at] = piece

    def groups(number):
        for first in range(number * run, (number + 1) * run, group):
            yield first, slice((first - number * run) * tall, (first - number * run + group) * tall)

    def flat(ref, *index):
        value = ref[index]
        return value.reshape(-1, wide)

    def near(ref, first, *index):
        return flat(ref, *index, slice(first, first + group))

    def put(ref, value, first, *index):
        ref[index + (slice(first, first + group),)] = value.reshape(group, tall, wide)

    def cut(slot, number, rows, value, count):
        for part, piece in enumerate(split(value, count)):
            parts_ref[slot, number, part * block + rows.start : part * block + rows.stop] = piece

    def multiply(slot, number, count, sampled):
        held = parts_ref[slot, number, : count * block]
        tops = rows_ref.shape[1] if sampled else block
        beside = jnp.concatenate([held[part * block : (part + 1) * block] for part in range(count)], axis=1)
        down = product(rows_ref[number, :tops, : count * block], held)
        product_ref[slot, number] = down[:block] + product(beside, wide_ref[: count * wide])
        if sampled:
            taken_ref[slot, number] = down[block:]

    def applied(slot, number, rows, first, ref, *index):
        total = (3.0 * whole_coeffs[0]) * near(ref, first, *index) + product_ref[slot, number, rows]
        pieces = []
        for z in range(first, first + group):
            piece = total[(z - first) * tall : (z - first + 1) * tall]
            for k in range(1, 5):
                for other in (z - k, z + k):
                    if 0 <= other < deep and other // run != z // run:
                        piece = piece + float(whole_coeffs[k]) * ref[index + (other,)]
            pieces.append(piece)
        return jnp.concatenate(pieces, axis=0) if len(pieces) > 1 else pieces[0]

    def start_incident(number):
        for first, rows in groups(number):
            cut(0, number, rows, near(field_ref, first, 1), 3)

    def step_incident(n, number):
        before, now, after = n % 4, (n + 1) % 4, (n + 2) % 4
        for first, rows in groups(number):
            drive = near(speed_ref, first) * applied(0, number, rows, first, field_ref, now)
            drive += near(force_ref, first, n)
            put(drive_ref, drive, first)
            following = 2.0 * near(field_ref, first, now) - near(field_ref, first, before) + drive
            put(field_ref, following, first, after)
            cut(0, number, rows, following, 3)
            if n == 0:
                for r in range(replicas):
                    wave = near(contrast_ref, first, r) * drive
                    put(wave_ref, wave, first, r, 0)
                    cut(1 + r, number, rows, wave, WAVE_PARTS)

    def step_wave(n, r, number):
        for first, rows in groups(number):
            following = (
                2.0 * near(wave_ref, first, r, n - 1)
                + near(speed_ref, first) * applied(1 + r, number, rows, first, wave_ref, r, n - 1)
                + near(contrast_ref, first, r) * near(drive_ref, first)
            )
            if n > 1:
                following -= near(wave_ref, first, r, n - 2)
            put(wave_ref, following, first, r, n)
            cut(1 + r, number, rows, following, WAVE_PARTS)

    at_z = pl.multiple_of(slab * deep_count, deep_count)
    at_y = pl.multiple_of(sub * tall_count, tall_count)
    at_x = pl.multiple_of(rep * part_width, part_width)

    def owned(ref, *index):
        here = index + (pl.ds(at_z, deep_count), pl.ds(at_y, tall_count), slice(None))
        return ref[here].reshape(own, wide)

    def chosen(slot, rows, count):
        total = None
        for number in range(runs):
            start = number * 3 * block
            held = parts_ref[slot, number, : count * block]
            term = product(last_ref[rows, start : start + count * block], held)
            total = term if total is None else total + term
        return total

    samples = [[None] * replicas for _ in range(STEPS)]
    each = range(runs)

    for number in each:
        start_incident(number)
    for number in each:
        multiply(0, number, 3, False)
    for number in each:
        for first, rows in groups(number):
            cut(1 + replicas, number, rows, near(speed_ref, first), 3)
    for number in each:
        step_incident(0, number)
    for n in (1, 2):
        work = [(multiply, (0, number, 3, False)) for number in each]
        after = [(step_incident, (n, number)) for number in each]
        for r in range(replicas):
            work += [(multiply, (1 + r, number, WAVE_PARTS, True)) for number in each]
            after += [(step_wave, (n, r, number)) for number in each]
        for i in range(len(work) + runs):
            if i < len(work):
                work[i][0](*work[i][1])
            if i == len(work) and n == STEPS - 2:
                incident_result = chosen(0, slice(None), 3)
            if i >= runs:
                after[i - runs][0](*after[i - runs][1])
        for r in range(replicas):
            samples[n - 1][r] = sum(taken_ref[1 + r, number] for number in each)

    wave_results = [chosen(1 + r, slice(None), WAVE_PARTS) for r in range(replicas)]
    receiver_rows = slice(own + receivers, own + 2 * receivers)
    speed = jnp.concatenate([owned(speed_ref), chosen(1 + replicas, receiver_rows, 3)], axis=0)

    def last_field(result, mine):
        return jnp.concatenate([mine, result[own + receivers :]], axis=0)

    def last_applied(result, here, count):
        total = (3.0 * whole_coeffs[0]) * here + result[: own + receivers]
        return total + product(jnp.concatenate(split(here, count), axis=1), wide_ref[: count * wide])

    column = lax.broadcasted_iota(jnp.int32, (receivers, 128), 1)
    mask = mask_ref[...]

    def recorded(n):
        total = jnp.zeros((receivers, 128), jnp.float32)
        for r in range(replicas):
            summed = jnp.sum(samples[n][r] * mask, axis=1, keepdims=True)
            total += jnp.where(column == n * replicas + r, summed, 0.0)
        return total

    now = last_field(incident_result, owned(field_ref, 0))
    waves = [last_field(wave_results[r], owned(wave_ref, r, 2)) for r in range(replicas)]
    incident_result = last_applied(incident_result, now, 3)
    wave_results = [last_applied(wave_results[r], waves[r], WAVE_PARTS) for r in range(replicas)]
    for r in range(replicas):
        samples[2][r] = waves[r][own:]
    gathered = recorded(0) + recorded(1) + recorded(2)
    drive = speed * incident_result + last_force_ref[...]
    slim_ref[...] = 2.0 * now[:own] - owned(field_ref, 3) + drive[:own]
    incident_ref[...] = slim_ref[:, pl.ds(at_x, part_width)].reshape(incident_ref.shape)
    send(incident_ref, outputs[0])
    for r in range(replicas):
        before = jnp.concatenate([owned(wave_ref, r, 1), samples[1][r]], axis=0)
        following = 2.0 * waves[r] - before + speed * wave_results[r] + last_contrast_ref[r] * drive
        scattered_ref[r] = following[:own].reshape(scattered_ref.shape[1:])
        send(scattered_ref.at[r], outputs[1].at[r])
        samples[3][r] = following[own:]
    gathered += recorded(3)
    traces_ref[...] = jnp.transpose(gathered)[: STEPS * replicas, :]
    send(traces_ref, outputs[2])
    for copy in copies:
        copy.wait()


def swapped(array, axis, distance):
    size = lax.axis_size(axis)
    return lax.ppermute(array, axis, [(i, i ^ distance) for i in range(size)])


def exchanged(own, deep_count, matrices, prepared):
    sent = own[: 3 * deep_count]
    beyond = {m: swapped(sent, "slab", m) for m in (1, 2)}
    late, matrices = lax.optimization_barrier((sent, matrices))
    beyond[3] = swapped(late, "slab", 3)
    near = jnp.concatenate([own[: 2 * deep_count], beyond[1]], axis=0)
    near_two, two_two = swapped(near, "rep", 1), swapped(beyond[2], "rep", 1)
    near_two, prepared = lax.optimization_barrier((near_two, prepared))
    three_two = swapped(beyond[3], "rep", 1)
    blocks = [
        jnp.concatenate([near, near_two, own[2 * deep_count :]], axis=0),
        jnp.concatenate([beyond[2], two_two], axis=0),
        jnp.concatenate([beyond[3], three_two], axis=0),
    ]
    blocks += [swapped(block, "sub", 1) for block in blocks]
    names = ("now", "prev", "courant")
    near_layout = [(name, 0) for name in names[:2]] + [(name, 1) for name in names]
    layouts = [[(name, x, z) for x in range(2) for name, z in near_layout]]
    layouts[0] += [("courant", x, 0) for x in range(2)]
    layouts += [[(name, x, z) for x in range(2) for name in names] for z in (2, 3)]
    layout = [
        (len(layouts) * y + number, i * deep_count, name, x, y, z)
        for y in range(2)
        for number, parts in enumerate(layouts)
        for i, (name, x, z) in enumerate(parts)
    ]
    return blocks, tuple(layout), (*prepared, *matrices)


def whole_shards(
    courant,
    incident_prev,
    incident_now,
    wavelet,
    source_z,
    source_y,
    source_x,
    replica_seeds,
    receiver_z,
    receiver_y,
    receiver_x,
):
    deep_count, tall_count, part_width = incident_now.shape
    wide = courant.shape[2]
    deep, tall = lax.axis_size("slab") * deep_count, lax.axis_size("sub") * tall_count
    rows = deep * tall
    replicas, receivers = replica_seeds.shape[0], receiver_z.shape[0]
    own_shape = (deep_count, tall_count, part_width)
    cube = (deep, tall, wide)
    last_rows = deep_count * tall_count + receivers
    block = min(rows, 256)
    vmem = pl.BlockSpec(memory_space=pltpu.VMEM)
    anywhere = pl.BlockSpec(memory_space=pltpu.HBM)

    def held(*shape, dtype=jnp.float32):
        return jax.ShapeDtypeStruct(shape, dtype)

    def call(kernel, out_shape, distant, arrays, scratch, out_space=vmem):
        return pl.pallas_call(
            kernel,
            out_shape=out_shape,
            in_specs=[anywhere] * len(distant) + [vmem] * len(arrays),
            out_specs=tuple(out_space for _ in out_shape),
            scratch_shapes=list(scratch),
            compiler_params=pltpu.CompilerParams(vmem_limit_bytes=24 * 2**20),
        )(*(pltpu.with_memory_space_constraint(a, pltpu.HBM) for a in distant), *arrays)

    given = (
        wavelet,
        source_z,
        source_y,
        source_x,
        replica_seeds,
        receiver_z,
        receiver_y,
        receiver_x,
    )
    prepared = call(
        functools.partial(prepare_kernel, own_shape[:2]),
        (
            held(replicas, *cube),
            held(STEPS - 1, *cube),
            held(replicas, last_rows, wide),
            held(last_rows, wide),
            held(rows // block, block + receivers, 3 * block, dtype=jnp.bfloat16),
            held(last_rows + receivers, 3 * rows, dtype=jnp.bfloat16),
            held(receivers, wide),
        ),
        given,
        (),
        (
            *(pltpu.SMEM(array.shape, array.dtype) for array in given),
            pltpu.SemaphoreType.DMA((len(given),)),
        ),
    )
    matrices = call(beside_kernel, (held(3 * wide, wide, dtype=jnp.bfloat16),), (), (), ())
    own = call(
        pack_kernel,
        (held(4 * deep_count, tall_count, part_width),),
        (incident_now, incident_prev, courant),
        (),
        (pltpu.SemaphoreType.DMA((4,)),),
    )[0]
    blocks, layout, prepared = exchanged(own, deep_count, matrices, prepared)
    incident_final, scattered_final, traces = call(
        functools.partial(step_kernel, layout, own_shape),
        (
            held(*own_shape),
            held(replicas, deep_count, tall_count, wide),
            held(STEPS * replicas, receivers),
        ),
        (),
        (*prepared, *blocks),
        (
            pltpu.VMEM((4,) + cube, jnp.float32),
            pltpu.VMEM(cube, jnp.float32),
            pltpu.VMEM(cube, jnp.float32),
            pltpu.VMEM((replicas, 3) + cube, jnp.float32),
            pltpu.VMEM((2 + replicas, rows // block, 3 * block, wide), jnp.bfloat16),
            pltpu.VMEM((1 + replicas, rows // block, block, wide), jnp.float32),
            pltpu.VMEM((1 + replicas, rows // block, receivers, wide), jnp.float32),
            pltpu.VMEM((deep_count * tall_count, wide), jnp.float32),
            pltpu.VMEM(own_shape, jnp.float32),
            pltpu.VMEM((replicas, deep_count, tall_count, wide), jnp.float32),
            pltpu.VMEM((STEPS * replicas, receivers), jnp.float32),
            pltpu.SemaphoreType.DMA((2 + replicas,)),
        ),
        anywhere,
    )
    return incident_final, scattered_final, traces.reshape(STEPS, replicas, receivers)


def solution(mesh):
    slabs, subs, reps = (mesh.shape[axis] for axis in ("slab", "sub", "rep"))

    def step(courant, *rest):
        deep, tall, _ = courant.shape
        paired = (slabs, subs, reps, mesh.shape["shot"]) == (4, 2, 2, 2)
        part_width = courant.shape[2] // reps
        fits = deep * tall <= GRID_ROWS and part_width % 128 == 0
        return jax.shard_map(
            whole_shards if paired and fits else halo_shards,
            mesh=mesh,
            in_specs=(
                P("slab", "sub", None),
                P(("shot", "slab"), "sub", "rep"),
                P(("shot", "slab"), "sub", "rep"),
                P(),
                P("shot"),
                P("shot"),
                P("shot"),
                P("rep"),
                P(),
                P(),
                P(),
            ),
            out_specs=(
                P(("shot", "slab"), "sub", "rep"),
                P("rep", ("shot", "slab"), "sub", None),
                P("shot", "rep", None),
            ),
            check_vma=False,
        )(courant, *rest)

    return step
```

```python
import functools

import jax
import jax.numpy as jnp
import numpy as np
from jax import lax
from jax.experimental import pallas as pl
from jax.experimental.pallas import tpu as pltpu
from jax.sharding import PartitionSpec as P

STEPS = 4
GRID_ROWS = 512
CHUNK = 2
WAVE_PARTS = 2


stencil_coeffs = (-205.0 / 72.0, 8.0 / 5.0, -1.0 / 5.0, 8.0 / 315.0, -1.0 / 560.0)
pert_scale = 0.2
whole_coeffs = (-14350, 8064, -1008, 128, -9)
coeff_scale = 5040.0


def padded_2(array, sides, width):
    for axis, dim in sides:
        size, length = (lax.axis_size(axis), array.shape[dim])
        up = [(i, (i + 1) % size) for i in range(size - 1)]
        down = [(j, i) for i, j in up]
        last = lax.slice_in_dim(array, length - width, length, axis=dim)
        first = lax.slice_in_dim(array, 0, width, axis=dim)
        before = lax.ppermute(last, axis, up)
        after = lax.ppermute(first, axis, down)
        array = jnp.concatenate([before, array, after], axis=dim)
    return array


def laplace(padded):
    deep_count = padded.shape[-3] - 8
    tall_count = padded.shape[-2] - 8
    wide_count = padded.shape[-1] - 8

    def window(shift_z, shift_y, shift_x):
        return padded[
            ...,
            4 + shift_z : 4 + shift_z + deep_count,
            4 + shift_y : 4 + shift_y + tall_count,
            4 + shift_x : 4 + shift_x + wide_count,
        ]

    summed = 3.0 * stencil_coeffs[0] * window(0, 0, 0)
    for offset in range(1, 5):
        couple = (
            window(offset, 0, 0)
            + window(-offset, 0, 0)
            + window(0, offset, 0)
            + window(0, -offset, 0)
            + window(0, 0, offset)
            + window(0, 0, -offset)
        )
        summed = summed + stencil_coeffs[offset] * couple
    return summed


def perturbation(seed_values, depth_coord, height_coord, width_coord):
    hashed = (
        seed_values[:, None, None, None] * 668265263
        + depth_coord[None, :, None, None] * 73856093
        + height_coord[None, None, :, None] * 19349663
        + width_coord[None, None, None, :] * 83492791
    )
    hashed = jnp.bitwise_xor(hashed, jnp.right_shift(hashed, 15))
    hashed = hashed * 1274126177
    hashed = jnp.bitwise_xor(hashed, jnp.right_shift(hashed, 13))
    fraction = jnp.bitwise_and(hashed, 65535).astype(jnp.float32) / 65535.0
    return pert_scale * (2.0 * fraction - 1.0)


def inject(field, amounts, where_z, where_y, where_x, start_z, start_y, start_x):
    local_z = where_z - start_z
    local_y = where_y - start_y
    local_x = where_x - start_x
    inside = (
        (local_z >= 0)
        & (local_z < field.shape[0])
        & (local_y >= 0)
        & (local_y < field.shape[1])
        & (local_x >= 0)
        & (local_x < field.shape[2])
    )
    clip_z = jnp.clip(local_z, 0, field.shape[0] - 1)
    clip_y = jnp.clip(local_y, 0, field.shape[1] - 1)
    clip_x = jnp.clip(local_x, 0, field.shape[2] - 1)
    return field.at[clip_z, clip_y, clip_x].add(jnp.where(inside, amounts, jnp.zeros_like(amounts)))


def sample(field, where_z, where_y, where_x, start_z, start_y):
    local_z = where_z - start_z
    local_y = where_y - start_y
    inside = (
        (local_z >= 0) & (local_z < field.shape[1]) & (local_y >= 0) & (local_y < field.shape[2])
    )
    clip_z = jnp.clip(local_z, 0, field.shape[1] - 1)
    clip_y = jnp.clip(local_y, 0, field.shape[2] - 1)
    picked = field[:, clip_z, clip_y, where_x]
    return jnp.where(inside[None, :], picked, jnp.zeros_like(picked))


def halo_shards(
    courant,
    incident_prev,
    incident_now,
    wavelet,
    source_z,
    source_y,
    source_x,
    replica_seeds,
    receiver_z,
    receiver_y,
    receiver_x,
):
    deep_count, tall_count, part_width = incident_now.shape
    full_width = courant.shape[2]
    start_z = lax.axis_index("slab") * deep_count
    start_y = lax.axis_index("sub") * tall_count
    start_x = lax.axis_index("rep") * part_width
    speed_square = courant * courant
    depth_coord = start_z + jnp.arange(deep_count, dtype=jnp.int32)
    height_coord = start_y + jnp.arange(tall_count, dtype=jnp.int32)
    width_coord = jnp.arange(full_width, dtype=jnp.int32)
    contrast = perturbation(replica_seeds, depth_coord, height_coord, width_coord)
    whole_prev, whole_now = (
        lax.all_gather(incident_prev, "rep", axis=2, tiled=True),
        lax.all_gather(incident_now, "rep", axis=2, tiled=True),
    )
    wave_prev = jnp.zeros(contrast.shape, jnp.float32)
    wave_now = jnp.zeros(contrast.shape, jnp.float32)
    recorded = []
    for step_index in range(STEPS):
        padded = padded_2(whole_now, (("slab", 0), ("sub", 1)), 4)
        padded = jnp.pad(padded, ((0, 0), (0, 0), (4, 4)))
        whole_next = 2.0 * whole_now - whole_prev + speed_square * laplace(padded)
        whole_next = inject(
            whole_next, wavelet[step_index], source_z, source_y, source_x, start_z, start_y, 0
        )
        wave_padded = padded_2(wave_now, (("slab", 1), ("sub", 2)), 4)
        wave_padded = jnp.pad(wave_padded, ((0, 0), (0, 0), (0, 0), (4, 4)))
        source_term = 2.0 * contrast * (whole_next - 2.0 * whole_now + whole_prev)
        whole_prev, whole_now = (whole_now, whole_next)
        wave_next = 2.0 * wave_now - wave_prev + speed_square * laplace(wave_padded) + source_term
        picked = sample(wave_next, receiver_z, receiver_y, receiver_x, start_z, start_y)
        picked = lax.psum(picked, ("slab", "sub"))
        recorded.append(picked)
        wave_prev, wave_now = (wave_now, wave_next)
    traces = jnp.stack(recorded)
    incident_final = lax.dynamic_slice_in_dim(whole_now, start_x, part_width, 2)
    return (incident_final, wave_now, traces)


def band(apart):
    value = jnp.zeros(apart.shape, jnp.float32)
    for k in range(1, 5):
        value = jnp.where(apart == k, float(whole_coeffs[k]), value)
    return value


def split(value, count):
    parts = []
    for part in range(count):
        parts.append(value.astype(jnp.bfloat16))
        if part < count - 1:
            value = value - parts[-1].astype(jnp.float32)
    return parts


def product(left, right):
    return jnp.dot(left, right, preferred_element_type=jnp.float32)


def across(row, column, tall):
    far_z = jnp.abs(lax.div(row, tall) - lax.div(column, tall))
    far_y = jnp.abs(lax.rem(row, tall) - lax.rem(column, tall))
    return band(jnp.where(far_y == 0, far_z, jnp.where(far_z == 0, far_y, 0)))


def doubled_contrast(cell, seed):
    hashed = cell + seed * 668265263
    hashed = hashed ^ (hashed >> 15)
    hashed = hashed * 1274126177
    hashed = hashed ^ (hashed >> 13)
    fraction = (hashed & 65535).astype(jnp.float32) / 65535.0
    return 2.0 * (pert_scale * (2.0 * fraction - 1.0))


def fetched(sources, targets, semaphores):
    copies = [
        pltpu.make_async_copy(source, target, semaphores.at[i])
        for i, (source, target) in enumerate(zip(sources, targets, strict=True))
    ]
    for copy in copies:
        copy.start()
    return copies


def pack_kernel(now_ref, prev_ref, courant_ref, own_ref, semaphores):
    layers, _, part_width = now_ref.shape
    rep = lax.axis_index("rep")
    sources = [now_ref, prev_ref]
    for x in range(2):
        at_x = pl.multiple_of((rep ^ x) * part_width, part_width)
        sources.append(courant_ref.at[:, :, pl.ds(at_x, part_width)])
    targets = [own_ref.at[pl.ds(i * layers, layers)] for i in range(4)]
    for copy in fetched(sources, targets, semaphores):
        copy.wait()


def beside_kernel(wide_ref):
    wide = wide_ref.shape[1]
    line = lax.broadcasted_iota(jnp.int32, (wide, wide), 0)
    beside = band(jnp.abs(line - lax.broadcasted_iota(jnp.int32, (wide, wide), 1)))
    for part in range(3):
        wide_ref[part * wide : (part + 1) * wide, :] = beside.astype(jnp.bfloat16)


def prepare_kernel(own_shape, *refs):
    given, outputs, held, semaphores = refs[:8], refs[8:15], refs[15:23], refs[23]
    contrast_ref, force_ref, last_contrast_ref, last_force_ref = outputs[:4]
    rows_ref, last_ref, mask_ref = outputs[4:]
    wavelet_ref, source_z_ref, source_y_ref, source_x_ref = held[:4]
    seeds_ref, receiver_z_ref, receiver_y_ref, receiver_x_ref = held[4:]
    copies = fetched(given, held, semaphores)
    deep, tall, wide = force_ref.shape[1:]
    rows = deep * tall
    runs, tops, block = rows_ref.shape[0], rows_ref.shape[1], rows_ref.shape[2] // 3
    receivers = mask_ref.shape[0]
    deep_count, tall_count = own_shape
    own = deep_count * tall_count
    replicas = seeds_ref.shape[0]
    sources = range(source_z_ref.shape[0])
    for copy in copies:
        copy.wait()
    z_of = lax.broadcasted_iota(jnp.int32, (deep, tall, wide), 0)
    y_of = lax.broadcasted_iota(jnp.int32, (deep, tall, wide), 1)
    x_of = lax.broadcasted_iota(jnp.int32, (deep, tall, wide), 2)
    cell = z_of * 73856093 + y_of * 19349663 + x_of * 83492791
    for r in range(replicas):
        contrast_ref[r] = doubled_contrast(cell, seeds_ref[r])
    lane = lax.broadcasted_iota(jnp.int32, (1, wide), 1)
    force_ref[...] = jnp.zeros_like(force_ref)
    for n in range(STEPS - 1):
        for k in sources:
            at = (n, source_z_ref[k], pl.ds(source_y_ref[k], 1), slice(None))
            force_ref[at] += jnp.where(lane == source_x_ref[k], wavelet_ref[n, k], 0.0)
    index = lax.broadcasted_iota(jnp.int32, (own + receivers, 1), 0)
    row = (lax.axis_index("slab") * deep_count + lax.div(index, tall_count)) * tall
    row += lax.axis_index("sub") * tall_count + lax.rem(index, tall_count)
    for j in range(receivers):
        row = jnp.where(index == own + j, receiver_z_ref[j] * tall + receiver_y_ref[j], row)
        mask_ref[pl.ds(j, 1), :] = jnp.where(lane == receiver_x_ref[j], 1.0, 0.0)
    cell = lax.div(row, tall) * 73856093 + lax.rem(row, tall) * 19349663 + lane * 83492791
    for r in range(replicas):
        last_contrast_ref[r] = doubled_contrast(cell, seeds_ref[r])
    force = jnp.zeros((own + receivers, wide), jnp.float32)
    for k in sources:
        here = (row == source_z_ref[k] * tall + source_y_ref[k]) & (lane == source_x_ref[k])
        force += jnp.where(here, wavelet_ref[STEPS - 1, k], 0.0)
    last_force_ref[...] = force
    column = lax.broadcasted_iota(jnp.int32, (1, rows), 1)
    taken = jnp.where(row[own:] == column, 1.0, 0.0)
    last = jnp.concatenate([across(row, column, tall), taken], axis=0).astype(jnp.bfloat16)
    line = lax.broadcasted_iota(jnp.int32, (block, 1), 0)
    inner = across(line, column[:, :block], tall).astype(jnp.bfloat16)
    for part in range(3):
        for run in range(runs):
            start = (3 * run + part) * block
            last_ref[:, start : start + block] = last[:, run * block : (run + 1) * block]
            here = (run, slice(0, block), slice(part * block, (part + 1) * block))
            rows_ref[here] = inner
            here = (run, slice(block, tops), slice(part * block, (part + 1) * block))
            rows_ref[here] = taken[:, run * block : (run + 1) * block].astype(jnp.bfloat16)


def step_kernel(
    layout,
    own_shape,
    contrast_ref,
    force_ref,
    last_contrast_ref,
    last_force_ref,
    rows_ref,
    last_ref,
    mask_ref,
    wide_ref,
    *refs,
):
    blocks, refs = refs[:-15], refs[-15:]
    outputs = refs[:3]
    field_ref, speed_ref, drive_ref, wave_ref, parts_ref, product_ref, taken_ref, slim_ref = refs[3:11]
    incident_ref, scattered_ref, traces_ref, semaphores = refs[11:]
    copies = []

    def send(source, target):
        copies.append(pltpu.make_async_copy(source, target, semaphores.at[len(copies)]))
        copies[-1].start()

    deep, tall, wide = speed_ref.shape
    deep_count, tall_count, part_width = own_shape
    own = deep_count * tall_count
    replicas = contrast_ref.shape[0]
    receivers = mask_ref.shape[0]
    runs, block = rows_ref.shape[0], rows_ref.shape[2] // 3
    run = block // tall
    group = min(run, CHUNK)
    slab, sub, rep = (lax.axis_index(axis) for axis in ("slab", "sub", "rep"))

    for number, layer, what, x, y, z in layout:
        half = rep ^ x
        at = (
            pl.ds(pl.multiple_of((slab ^ z) * deep_count, deep_count), deep_count),
            pl.ds(pl.multiple_of((sub ^ y) * tall_count, tall_count), tall_count),
            pl.ds(pl.multiple_of(half * part_width, part_width), part_width),
        )
        piece = blocks[number][layer : layer + deep_count]
        if what == "courant":
            speed_ref[at] = piece * piece * (1.0 / coeff_scale)
        else:
            field_ref[(("prev", "now").index(what),) + at] = piece

    def groups(number):
        for first in range(number * run, (number + 1) * run, group):
            yield first, slice((first - number * run) * tall, (first - number * run + group) * tall)

    def flat(ref, *index):
        value = ref[index]
        return value.reshape(-1, wide)

    def near(ref, first, *index):
        return flat(ref, *index, slice(first, first + group))

    def put(ref, value, first, *index):
        ref[index + (slice(first, first + group),)] = value.reshape(group, tall, wide)

    def cut(slot, number, rows, value, count):
        for part, piece in enumerate(split(value, count)):
            parts_ref[slot, number, part * block + rows.start : part * block + rows.stop] = piece

    def multiply(slot, number, count, sampled):
        held = parts_ref[slot, number, : count * block]
        tops = rows_ref.shape[1] if sampled else block
        beside = jnp.concatenate([held[part * block : (part + 1) * block] for part in range(count)], axis=1)
        down = product(rows_ref[number, :tops, : count * block], held)
        product_ref[slot, number] = down[:block] + product(beside, wide_ref[: count * wide])
        if sampled:
            taken_ref[slot, number] = down[block:]

    def applied(slot, number, rows, first, ref, *index):
        total = (3.0 * whole_coeffs[0]) * near(ref, first, *index) + product_ref[slot, number, rows]
        pieces = []
        for z in range(first, first + group):
            piece = total[(z - first) * tall : (z - first + 1) * tall]
            for k in range(1, 5):
                for other in (z - k, z + k):
                    if 0 <= other < deep and other // run != z // run:
                        piece = piece + float(whole_coeffs[k]) * ref[index + (other,)]
            pieces.append(piece)
        return jnp.concatenate(pieces, axis=0) if len(pieces) > 1 else pieces[0]

    def start_incident(number):
        for first, rows in groups(number):
            cut(0, number, rows, near(field_ref, first, 1), 3)

    def step_incident(n, number):
        before, now, after = n % 4, (n + 1) % 4, (n + 2) % 4
        for first, rows in groups(number):
            drive = near(speed_ref, first) * applied(0, number, rows, first, field_ref, now)
            drive += near(force_ref, first, n)
            put(drive_ref, drive, first)
            following = 2.0 * near(field_ref, first, now) - near(field_ref, first, before) + drive
            put(field_ref, following, first, after)
            cut(0, number, rows, following, 3)
            if n == 0:
                for r in range(replicas):
                    wave = near(contrast_ref, first, r) * drive
                    put(wave_ref, wave, first, r, 0)
                    cut(1 + r, number, rows, wave, WAVE_PARTS)

    def step_wave(n, r, number):
        for first, rows in groups(number):
            following = (
                2.0 * near(wave_ref, first, r, n - 1)
                + near(speed_ref, first) * applied(1 + r, number, rows, first, wave_ref, r, n - 1)
                + near(contrast_ref, first, r) * near(drive_ref, first)
            )
            if n > 1:
                following -= near(wave_ref, first, r, n - 2)
            put(wave_ref, following, first, r, n)
            cut(1 + r, number, rows, following, WAVE_PARTS)

    at_z = pl.multiple_of(slab * deep_count, deep_count)
    at_y = pl.multiple_of(sub * tall_count, tall_count)
    at_x = pl.multiple_of(rep * part_width, part_width)

    def owned(ref, *index):
        here = index + (pl.ds(at_z, deep_count), pl.ds(at_y, tall_count), slice(None))
        return ref[here].reshape(own, wide)

    def chosen(slot, rows, count):
        total = None
        for number in range(runs):
            start = number * 3 * block
            held = parts_ref[slot, number, : count * block]
            term = product(last_ref[rows, start : start + count * block], held)
            total = term if total is None else total + term
        return total

    samples = [[None] * replicas for _ in range(STEPS)]
    each = range(runs)

    for number in each:
        start_incident(number)
    for number in each:
        multiply(0, number, 3, False)
    for number in each:
        for first, rows in groups(number):
            cut(1 + replicas, number, rows, near(speed_ref, first), 3)
    for number in each:
        step_incident(0, number)
    for n in (1, 2):
        work = [(multiply, (0, number, 3, False)) for number in each]
        after = [(step_incident, (n, number)) for number in each]
        for r in range(replicas):
            work += [(multiply, (1 + r, number, WAVE_PARTS, True)) for number in each]
            after += [(step_wave, (n, r, number)) for number in each]
        for i in range(len(work) + runs):
            if i < len(work):
                work[i][0](*work[i][1])
            if i == len(work) and n == STEPS - 2:
                incident_result = chosen(0, slice(None), 3)
            if i >= runs:
                after[i - runs][0](*after[i - runs][1])
        for r in range(replicas):
            samples[n - 1][r] = sum(taken_ref[1 + r, number] for number in each)

    wave_results = [chosen(1 + r, slice(None), WAVE_PARTS) for r in range(replicas)]
    receiver_rows = slice(own + receivers, own + 2 * receivers)
    speed = jnp.concatenate([owned(speed_ref), chosen(1 + replicas, receiver_rows, 3)], axis=0)

    def last_field(result, mine):
        return jnp.concatenate([mine, result[own + receivers :]], axis=0)

    def last_applied(result, here, count):
        total = (3.0 * whole_coeffs[0]) * here + result[: own + receivers]
        return total + product(jnp.concatenate(split(here, count), axis=1), wide_ref[: count * wide])

    column = lax.broadcasted_iota(jnp.int32, (receivers, 128), 1)
    mask = mask_ref[...]

    def recorded(n):
        total = jnp.zeros((receivers, 128), jnp.float32)
        for r in range(replicas):
            summed = jnp.sum(samples[n][r] * mask, axis=1, keepdims=True)
            total += jnp.where(column == n * replicas + r, summed, 0.0)
        return total

    now = last_field(incident_result, owned(field_ref, 0))
    waves = [last_field(wave_results[r], owned(wave_ref, r, 2)) for r in range(replicas)]
    incident_result = last_applied(incident_result, now, 3)
    wave_results = [last_applied(wave_results[r], waves[r], WAVE_PARTS) for r in range(replicas)]
    for r in range(replicas):
        samples[2][r] = waves[r][own:]
    gathered = recorded(0) + recorded(1) + recorded(2)
    drive = speed * incident_result + last_force_ref[...]
    slim_ref[...] = 2.0 * now[:own] - owned(field_ref, 3) + drive[:own]
    incident_ref[...] = slim_ref[:, pl.ds(at_x, part_width)].reshape(incident_ref.shape)
    send(incident_ref, outputs[0])
    for r in range(replicas):
        before = jnp.concatenate([owned(wave_ref, r, 1), samples[1][r]], axis=0)
        following = 2.0 * waves[r] - before + speed * wave_results[r] + last_contrast_ref[r] * drive
        scattered_ref[r] = following[:own].reshape(scattered_ref.shape[1:])
        send(scattered_ref.at[r], outputs[1].at[r])
        samples[3][r] = following[own:]
    gathered += recorded(3)
    traces_ref[...] = jnp.transpose(gathered)[: STEPS * replicas, :]
    send(traces_ref, outputs[2])
    for copy in copies:
        copy.wait()


def swapped(array, axis, distance):
    size = lax.axis_size(axis)
    return lax.ppermute(array, axis, [(i, i ^ distance) for i in range(size)])


def exchanged(own, deep_count, matrices, prepared):
    sent = own[: 3 * deep_count]
    beyond = {m: swapped(sent, "slab", m) for m in (1, 2)}
    late, matrices = lax.optimization_barrier((sent, matrices))
    beyond[3] = swapped(late, "slab", 3)
    near = jnp.concatenate([own[: 2 * deep_count], beyond[1]], axis=0)
    near_two, two_two = swapped(near, "rep", 1), swapped(beyond[2], "rep", 1)
    line = jnp.concatenate([own[2 * deep_count :], near, near_two], axis=0)
    line, prepared = lax.optimization_barrier((line, prepared))
    three_two = swapped(beyond[3], "rep", 1)
    blocks = [
        line,
        jnp.concatenate([beyond[2], two_two], axis=0),
        jnp.concatenate([three_two, beyond[3]], axis=0),
    ]
    blocks += [swapped(block, "sub", 1) for block in blocks]
    names = ("now", "prev", "courant")
    near_layout = [(name, 0) for name in names[:2]] + [(name, 1) for name in names]
    layouts = [[("courant", x, 0) for x in range(2)]]
    layouts[0] += [(name, x, z) for x in range(2) for name, z in near_layout]
    layouts += [[(name, x, 2) for x in (0, 1) for name in names]]
    layouts += [[(name, x, 3) for x in (1, 0) for name in names]]
    layout = [
        (len(layouts) * y + number, i * deep_count, name, x, y, z)
        for y in range(2)
        for number, parts in enumerate(layouts)
        for i, (name, x, z) in enumerate(parts)
    ]
    return blocks, tuple(layout), (*prepared, *matrices)


def whole_shards(
    courant,
    incident_prev,
    incident_now,
    wavelet,
    source_z,
    source_y,
    source_x,
    replica_seeds,
    receiver_z,
    receiver_y,
    receiver_x,
):
    deep_count, tall_count, part_width = incident_now.shape
    wide = courant.shape[2]
    deep, tall = lax.axis_size("slab") * deep_count, lax.axis_size("sub") * tall_count
    rows = deep * tall
    replicas, receivers = replica_seeds.shape[0], receiver_z.shape[0]
    own_shape = (deep_count, tall_count, part_width)
    cube = (deep, tall, wide)
    last_rows = deep_count * tall_count + receivers
    block = min(rows, 256)
    vmem = pl.BlockSpec(memory_space=pltpu.VMEM)
    anywhere = pl.BlockSpec(memory_space=pltpu.HBM)

    def held(*shape, dtype=jnp.float32):
        return jax.ShapeDtypeStruct(shape, dtype)

    def call(kernel, out_shape, distant, arrays, scratch, out_space=vmem):
        return pl.pallas_call(
            kernel,
            out_shape=out_shape,
            in_specs=[anywhere] * len(distant) + [vmem] * len(arrays),
            out_specs=tuple(out_space for _ in out_shape),
            scratch_shapes=list(scratch),
            compiler_params=pltpu.CompilerParams(vmem_limit_bytes=24 * 2**20),
        )(*(pltpu.with_memory_space_constraint(a, pltpu.HBM) for a in distant), *arrays)

    given = (
        wavelet,
        source_z,
        source_y,
        source_x,
        replica_seeds,
        receiver_z,
        receiver_y,
        receiver_x,
    )
    prepared = call(
        functools.partial(prepare_kernel, own_shape[:2]),
        (
            held(replicas, *cube),
            held(STEPS - 1, *cube),
            held(replicas, last_rows, wide),
            held(last_rows, wide),
            held(rows // block, block + receivers, 3 * block, dtype=jnp.bfloat16),
            held(last_rows + receivers, 3 * rows, dtype=jnp.bfloat16),
            held(receivers, wide),
        ),
        given,
        (),
        (
            *(pltpu.SMEM(array.shape, array.dtype) for array in given),
            pltpu.SemaphoreType.DMA((len(given),)),
        ),
    )
    matrices = call(beside_kernel, (held(3 * wide, wide, dtype=jnp.bfloat16),), (), (), ())
    own = call(
        pack_kernel,
        (held(4 * deep_count, tall_count, part_width),),
        (incident_now, incident_prev, courant),
        (),
        (pltpu.SemaphoreType.DMA((4,)),),
    )[0]
    blocks, layout, prepared = exchanged(own, deep_count, matrices, prepared)
    incident_final, scattered_final, traces = call(
        functools.partial(step_kernel, layout, own_shape),
        (
            held(*own_shape),
            held(replicas, deep_count, tall_count, wide),
            held(STEPS * replicas, receivers),
        ),
        (),
        (*prepared, *blocks),
        (
            pltpu.VMEM((4,) + cube, jnp.float32),
            pltpu.VMEM(cube, jnp.float32),
            pltpu.VMEM(cube, jnp.float32),
            pltpu.VMEM((replicas, 3) + cube, jnp.float32),
            pltpu.VMEM((2 + replicas, rows // block, 3 * block, wide), jnp.bfloat16),
            pltpu.VMEM((1 + replicas, rows // block, block, wide), jnp.float32),
            pltpu.VMEM((1 + replicas, rows // block, receivers, wide), jnp.float32),
            pltpu.VMEM((deep_count * tall_count, wide), jnp.float32),
            pltpu.VMEM(own_shape, jnp.float32),
            pltpu.VMEM((replicas, deep_count, tall_count, wide), jnp.float32),
            pltpu.VMEM((STEPS * replicas, receivers), jnp.float32),
            pltpu.SemaphoreType.DMA((2 + replicas,)),
        ),
        anywhere,
    )
    return incident_final, scattered_final, traces.reshape(STEPS, replicas, receivers)


def solution(mesh):
    slabs, subs, reps = (mesh.shape[axis] for axis in ("slab", "sub", "rep"))

    def step(courant, *rest):
        deep, tall, _ = courant.shape
        paired = (slabs, subs, reps, mesh.shape["shot"]) == (4, 2, 2, 2)
        part_width = courant.shape[2] // reps
        fits = deep * tall <= GRID_ROWS and part_width % 128 == 0
        return jax.shard_map(
            whole_shards if paired and fits else halo_shards,
            mesh=mesh,
            in_specs=(
                P("slab", "sub", None),
                P(("shot", "slab"), "sub", "rep"),
                P(("shot", "slab"), "sub", "rep"),
                P(),
                P("shot"),
                P("shot"),
                P("shot"),
                P("rep"),
                P(),
                P(),
                P(),
            ),
            out_specs=(
                P(("shot", "slab"), "sub", "rep"),
                P("rep", ("shot", "slab"), "sub", None),
                P("shot", "rep", None),
            ),
            check_vma=False,
        )(courant, *rest)

    return step
```
